512 devices in a mesh: dp: 64 (over x, z), mp: 8 (over y, core).
Axes of the slice: x: 4, y: 4, z: 16, core: 2. Of those that a mesh axis runs over, the one named last changes fastest.
Arguments:
- partial_grads: bfloat16 [64, 16, 512, 512], P('dp', None, 'mp'), may hold values from -2 to 2
- owner_slot: int32 [16], replicated, may hold values from 0 to 15, each once
- extent: int32 [16, 2], replicated, may hold values from 128 to 512, as said below
- left_roots: bfloat16 [16, 512, 512], P('mp')
- right_roots: bfloat16 [16, 512, 512], P('mp', None, 'dp')
- momentum: float32 [16, 512, 512], P('mp', None, 'dp'), may hold values from -4 to 4
- master: float32 [16, 512, 512], P('mp', None, 'dp'), may hold values from -6 to 6
Outputs:
- new_momentum: float32 [16, 512, 512], P('mp', None, 'dp')
- new_master: float32 [16, 512, 512], P('mp', None, 'dp')
- weights: bfloat16 [16, 512, 512], P(None, 'mp')
The draws below stay inside these ranges and needn't reach their ends.
Inputs may be any that keep to these rules, and one draw needn't show every extreme that they name: owner_slot is a permutation of 0 to 15. `extent`: some block has both bounds equal to 512.
All inputs are finite; a program needn't handle non-finite values.
Results may differ from the reference program's by a relative error of at most 0.0035.
Values may be sent and summed in bfloat16 or wider, within the bound.
No kernel may reach another device: no remote copies, remote signals or barrier semaphores. Data moves between devices by JAX's collectives and lax.ppermute only.
A program may use at most 64 MiB of HBM per device.

```python
import math
import jax
import jax.numpy as jnp
from jax import lax

B = 512
W = 16
N_DP = 64


def draw_extent(key, part):
    key = jax.random.fold_in(key, 7)
    first, second = jax.random.split(key)
    values = jax.random.randint(first, (W, 2), B // 4, B + 1, dtype=jnp.int32)
    where = jax.random.randint(second, (), 0, W, dtype=jnp.int32)
    chosen = (jnp.arange(W, dtype=jnp.int32) == where)[:, None]
    return jnp.where(chosen, B, values).astype(jnp.int32)


def shape_root(key, noise):
    diagonal_part = jnp.exp(jax.random.uniform(key, (W, B), jnp.float32, -0.7, 0.7))
    symmetric = (noise + jnp.swapaxes(noise, 1, 2)) * (0.3 / math.sqrt(2.0 * B))
    identity = (jnp.arange(B)[:, None] == jnp.arange(B)[None, :]).astype(jnp.float32)
    return (symmetric + identity[None] * diagonal_part[:, :, None]).astype(jnp.bfloat16)


def draw_left_roots(key, part):
    key = jax.random.fold_in(key, 11)
    first, second = jax.random.split(key)
    noise = jax.random.normal(second, (W, B, B), jnp.float32)
    return shape_root(first, noise)


def draw_right_roots(key, part):
    key = jax.random.fold_in(key, 13)
    first, second = jax.random.split(key)
    noise = jax.random.normal(second, (W, B, B), jnp.float32)
    return shape_root(first, noise)


def levels(own_key, dims, cuts, least, high):
    def one(dim, parts):
        steps = jax.random.uniform(jax.random.fold_in(jax.random.fold_in(own_key, 6), dim), (parts,), jnp.float32, least / len(cuts), high / len(cuts))
        return jnp.repeat(jnp.exp(steps), dims[dim] // parts).reshape((-1,) + (1,) * (len(dims) - dim - 1))

    level = one(*cuts[0])
    for cut in cuts[1:]:
        level = level * one(*cut)
    return level


def normal_values(rng, dims, width, reach, cuts=(), held_as=jnp.bfloat16):
    array = width * jax.random.normal(rng, dims, jnp.float32)
    if cuts:
        array = array * levels(rng, dims, cuts, -0.22, 0.18)
    return jnp.clip(array, -reach, reach).astype(held_as)


def setup_inputs(seed: int = 0) -> dict:
    seeds = jax.random.split(jax.random.key(seed), 8)
    partial_grads = normal_values(seeds[0], (N_DP, W, B, B), 0.125, 2.0, ((0, 64), (2, 8)))
    owner_slot = jax.random.permutation(seeds[1], W).astype(jnp.int32)
    extent = draw_extent(jax.random.fold_in(seeds[7], 71), 0)
    left_roots = draw_left_roots(jax.random.fold_in(seeds[7], 71), 0)
    right_roots = draw_right_roots(jax.random.fold_in(seeds[7], 71), 0)
    momentum = normal_values(seeds[5], (W, B, B), 0.5, 4.0, ((0, 8), (2, 64)), jnp.float32)
    master = normal_values(seeds[6], (W, B, B), 1.0, 6.0, ((0, 8), (2, 64)), jnp.float32)
    return dict(partial_grads=partial_grads, owner_slot=owner_slot, extent=extent, left_roots=left_roots, right_roots=right_roots, momentum=momentum, master=master)


epsilon = 1e-06
beta_decay = 0.9
step_rate = 0.5

def reference(partial_grads, owner_slot, extent, left_roots, right_roots, momentum, master):

    def accumulate(carry, piece):
        return (carry + piece.astype(jnp.float32), None)
    total, _ = lax.scan(accumulate, jnp.zeros(partial_grads.shape[1:], jnp.float32), partial_grads)
    slots = jnp.arange(W, dtype=jnp.int32)
    match = owner_slot[None, :] == slots[:, None]
    order = lax.optimization_barrier(jnp.sum(jnp.where(match, slots[None, :], 0), axis=1)).astype(jnp.int32)
    by_slot = jnp.take(total, order, axis=0)
    bounds = jnp.take(extent, order, axis=0)
    positions = jnp.arange(B, dtype=jnp.int32)
    row_mask = (positions[None, :] < bounds[:, 0:1]).astype(jnp.float32)
    col_mask = (positions[None, :] < bounds[:, 1:2]).astype(jnp.float32)
    mask = row_mask[:, :, None] * col_mask[:, None, :]
    grad = by_slot * mask
    grad_low = grad.astype(jnp.bfloat16)
    right_side = jnp.einsum('kij,kjc->kic', grad_low.astype(jnp.float32), right_roots.astype(jnp.float32)).astype(jnp.bfloat16)
    precond = jnp.einsum('kij,kjc->kic', left_roots.astype(jnp.float32), right_side.astype(jnp.float32))
    grad_sq = lax.optimization_barrier(jnp.sum(grad * grad, axis=(1, 2)))
    pre_sq = lax.optimization_barrier(jnp.sum(precond * precond, axis=(1, 2)))
    scale = jnp.sqrt(grad_sq / (pre_sq + epsilon))
    new_momentum = beta_decay * momentum + scale[:, None, None] * precond * mask
    new_master = master - step_rate * new_momentum
    weights = jnp.take(new_master, owner_slot, axis=0).astype(jnp.bfloat16)
    return (new_momentum, new_master, weights)
```

```python
import jax
import jax.numpy as jnp
from jax import lax
from jax.sharding import Mesh, PartitionSpec as P

epsilon = 1e-06
beta_decay = 0.9
step_rate = 0.5
f32 = jnp.float32
bf16 = jnp.bfloat16


def split_low(value):
    high = lax.reduce_precision(value, 8, 7)
    return high.astype(bf16), (value - high).astype(bf16)


def split3(value):
    high = lax.reduce_precision(value, 8, 7)
    middle = lax.reduce_precision(value - high, 8, 7)
    return high.astype(bf16), middle.astype(bf16), (value - high - middle).astype(bf16)


def make_local(nx, nz, nm):
    def local(partial_grads, owner_slot, extent, left_roots, right_roots, momentum, master):
        blocks = partial_grads.shape[1]
        rows = partial_grads.shape[2]
        width = partial_grads.shape[3]
        owned = left_roots.shape[0]
        slab = right_roots.shape[2]
        cols = width // nx
        band = width // nz
        x, z, m = lax.axis_index("x"), lax.axis_index("z"), lax.axis_index("mp")
        slots = jnp.arange(blocks, dtype=jnp.int32)
        match = owner_slot[None, :] == slots[:, None]
        order = jnp.sum(jnp.where(match, slots[None, :], 0), axis=1)
        bounds_all = jnp.sum(jnp.where(match[:, :, None], extent[None, :, :], 0), axis=1)
        bounds = lax.dynamic_slice_in_dim(bounds_all, m * owned, owned, 0)
        row_ids = jnp.arange(width, dtype=jnp.int32)

        base_t = jnp.swapaxes(master - (step_rate * beta_decay) * momentum, 1, 2)
        high, low = split_low(base_t)
        right_t = jnp.swapaxes(right_roots, 1, 2)
        mine = jnp.concatenate([right_t, high, low, jnp.zeros_like(high)], axis=0)
        parts = lax.all_gather(mine, "z", axis=0, tiled=False)
        parts = jnp.swapaxes(parts, 0, 1).reshape(4 * owned, cols, width)
        right_cols_t = parts[:owned]
        base_cols = jnp.swapaxes(
            parts[owned : 2 * owned].astype(f32) + parts[2 * owned : 3 * owned].astype(f32), 1, 2
        )

        send = jnp.take(partial_grads[0], order, axis=0)
        send = send.reshape(nm * owned, rows, nx, cols).transpose(2, 0, 1, 3)
        send = send.reshape(nx * nm, owned, rows, cols)
        got = lax.all_to_all(send, ("x", "mp"), split_axis=0, concat_axis=0, tiled=True)
        got = got.reshape(nx, nm, owned, rows, cols)
        part = got[0].astype(f32)
        for i in range(1, nx):
            part = part + got[i].astype(f32)
        part = part.reshape(nm, owned, rows // band, band, cols).transpose(0, 2, 1, 3, 4)
        part = part.reshape(nz, owned, band, cols)
        pieces = lax.all_to_all(part, "z", split_axis=0, concat_axis=0, tiled=True)
        total = jnp.sum(pieces, axis=0)
        band_rows = z * band + jnp.arange(band, dtype=jnp.int32)
        band_cols = x * cols + jnp.arange(cols, dtype=jnp.int32)
        row_ok = band_rows[None, :, None] < bounds[:, 0][:, None, None]
        col_ok = band_cols[None, None, :] < bounds[:, 1][:, None, None]
        grad = jnp.where(row_ok & col_ok, total, 0.0)
        sq_piece = jnp.sum(grad * grad, axis=(1, 2))
        grad_low = grad.astype(bf16)
        spread = jnp.broadcast_to(grad_low[None], (nx,) + grad_low.shape)
        all_cols = lax.all_to_all(spread, "x", split_axis=0, concat_axis=0, tiled=True)
        grad_rows = all_cols.transpose(1, 2, 0, 3).reshape(owned, band, width)
        right_side = jnp.einsum(
            "kij,kcj->kic", grad_rows, right_cols_t, preferred_element_type=f32
        ).astype(bf16)
        extra = jnp.stack(split3(sq_piece), axis=0).reshape(3 * owned)
        extra = jnp.broadcast_to(extra[:, None], (3 * owned, cols))
        extra = jnp.pad(extra, ((0, 16 - 3 * owned), (0, 0)))
        packed = jnp.concatenate([right_side.reshape(owned * band, cols), extra], axis=0)
        spread = jnp.broadcast_to(packed[None], (nz,) + packed.shape)
        bands = lax.all_to_all(spread, "z", split_axis=0, concat_axis=0, tiled=True)
        sq = bands[:, owned * band : owned * band + 3 * owned, 0].astype(f32)
        grad_sq = jnp.sum(sq.reshape(nz, 3, owned), axis=(0, 1))
        side = bands[:, : owned * band].reshape(nz, owned, band, cols)
        side = side.transpose(1, 0, 2, 3).reshape(owned, width, cols)
        precond = jnp.einsum("kij,kjc->kic", left_roots, side, preferred_element_type=f32)
        pre_sq = jnp.sum(precond * precond, axis=(1, 2))
        grad_sq, pre_sq = lax.psum(jnp.stack([grad_sq, pre_sq]), "x")
        scale = jnp.sqrt(grad_sq / (pre_sq + epsilon))
        mask = (row_ids[None, :, None] < bounds[:, 0][:, None, None]) & col_ok
        step = jnp.where(mask, scale[:, None, None] * precond, 0.0)
        fresh = (base_cols - step_rate * step).astype(bf16)
        fresh = fresh.reshape(owned, nm, rows, cols).transpose(1, 0, 2, 3)
        fresh = jnp.broadcast_to(fresh[None], (nx,) + fresh.shape)
        fresh = fresh.reshape(nx * nm, owned, rows, cols)
        back = lax.all_to_all(fresh, ("x", "mp"), split_axis=0, concat_axis=0, tiled=True)
        back = back.reshape(nx, blocks, rows, cols)
        weights = jnp.take(back, owner_slot, axis=1)
        weights = weights.transpose(1, 2, 0, 3).reshape(blocks, rows, width)

        own_step = lax.dynamic_slice_in_dim(step, z * slab, slab, 2)
        new_momentum = beta_decay * momentum + own_step
        new_master = master - step_rate * new_momentum
        return (new_momentum, new_master, weights)

    return local


def solution(mesh):
    nm = mesh.shape["mp"]
    nz = 16 if mesh.shape["dp"] == 64 else mesh.shape["dp"] // 2
    nx = mesh.shape["dp"] // nz
    fine = Mesh(mesh.devices.reshape(nx, nz, nm), ("x", "z", "mp"))
    slab_spec = P("mp", None, ("x", "z"))
    return jax.shard_map(
        make_local(nx, nz, nm),
        mesh=fine,
        in_specs=(
            P(("x", "z"), None, "mp", None),
            P(),
            P(),
            P("mp", None, None),
            slab_spec,
            slab_spec,
            slab_spec,
        ),
        out_specs=(slab_spec, slab_spec, P(None, "mp", None)),
        check_vma=False,
    )
```

```python
import jax
import jax.numpy as jnp
from jax import lax
from jax.sharding import Mesh, PartitionSpec as P

epsilon = 1e-06
beta_decay = 0.9
step_rate = 0.5
f32 = jnp.float32
bf16 = jnp.bfloat16


def split_low(value):
    high = lax.reduce_precision(value, 8, 7)
    return high.astype(bf16), (value - high).astype(bf16)


def exchange(value, axes):
    return lax.all_to_all(value, axes, split_axis=0, concat_axis=0, tiled=True)


def spread(value, count):
    return jnp.broadcast_to(value[None], (count,) + value.shape)


def make_local(nx, nzh, nzl, nm):
    ng = nx * nzl
    group = ("x", "zl")
    wide = ("x", "zl", "mp")

    def gather_along(value):
        zh = lax.axis_index("zh")
        held = value[None]
        stride = nzh // 2
        while stride:
            pairs = [(i, i ^ stride) for i in range(nzh)]
            other = lax.ppermute(held, "zh", pairs)
            first = (zh & stride) == 0
            low = jnp.where(first, held, other)
            high = jnp.where(first, other, held)
            held = jnp.stack([low, high], axis=1).reshape((-1,) + value.shape)
            stride //= 2
        return held

    def local(partial_grads, owner_slot, extent, left_roots, right_roots, momentum, master):
        blocks = partial_grads.shape[1]
        rows = partial_grads.shape[2]
        width = partial_grads.shape[3]
        owned = left_roots.shape[0]
        slab = right_roots.shape[2]
        cols = width // nx
        half = rows // nzl
        mine_cols = slab * nzh
        x, zh, zl, m = (lax.axis_index(a) for a in ("x", "zh", "zl", "mp"))
        slots = jnp.arange(blocks, dtype=jnp.int32)
        match = owner_slot[None, :] == slots[:, None]
        order = jnp.sum(jnp.where(match, slots[None, :], 0), axis=1)
        bounds_all = jnp.sum(jnp.where(match[:, :, None], extent[None, :, :], 0), axis=1)
        bounds = lax.dynamic_slice_in_dim(bounds_all, m * owned, owned, 0)

        base_t = jnp.swapaxes(master - (step_rate * beta_decay) * momentum, 1, 2)
        high, low = split_low(base_t)
        right_t = jnp.swapaxes(right_roots, 1, 2)
        mine = jnp.concatenate([right_t, high, low], axis=0)
        parts = gather_along(mine)
        parts = jnp.swapaxes(parts, 0, 1).reshape(3 * owned, mine_cols, width)
        right_cols_t = parts[:owned]
        base_cols = parts[owned : 2 * owned].astype(f32) + parts[2 * owned :].astype(f32)
        base_cols = base_cols.reshape(owned * mine_cols, width).T

        send = jnp.take(partial_grads[0], order, axis=0)
        send = send.reshape(nm, owned, nzl, half, nx, cols).transpose(4, 2, 0, 1, 3, 5)
        got = exchange(send.reshape(ng * nm, owned, half, cols), wide)
        got = got.reshape(ng, nm, owned, half, cols)
        part = got[0].astype(f32)
        for i in range(1, ng):
            part = part + got[i].astype(f32)
        pieces = exchange(part, "zh")
        total = jnp.sum(pieces, axis=0)
        piece_rows = zh * rows + zl * half + jnp.arange(half, dtype=jnp.int32)
        piece_cols = x * cols + jnp.arange(cols, dtype=jnp.int32)
        row_ok = piece_rows[None, :, None] < bounds[:, 0][:, None, None]
        col_ok = piece_cols[None, None, :] < bounds[:, 1][:, None, None]
        grad = jnp.where(row_ok & col_ok, total, 0.0)
        sq_piece = jnp.sum(grad * grad, axis=(1, 2))
        all_cols = exchange(spread(grad.astype(bf16), ng), group)
        all_cols = all_cols.reshape(nx, nzl, owned, half, cols)
        grad_rows = all_cols.transpose(2, 1, 3, 0, 4).reshape(owned, rows, width)
        right_side = jnp.einsum(
            "kij,kcj->ikc", grad_rows, right_cols_t, preferred_element_type=f32
        ).astype(bf16)
        sq_high = lax.reduce_precision(sq_piece, 8, 7)
        sq_middle = lax.reduce_precision(sq_piece - sq_high, 8, 7)
        sq_low = sq_piece - sq_high - sq_middle
        extra = jnp.concatenate([sq_high, sq_middle, sq_low]).astype(bf16)
        extra = jnp.broadcast_to(extra[:, None], (3 * owned, owned * mine_cols))
        extra = jnp.pad(extra, ((0, 16 - 3 * owned), (0, 0)))
        packed = jnp.concatenate([right_side.reshape(rows, owned * mine_cols), extra], axis=0)
        bands = exchange(spread(packed, nzh), "zh")
        sq = bands[:, rows : rows + 3 * owned, 0].astype(f32)
        grad_sq = jnp.sum(sq.reshape(nzh, 3, owned), axis=(0, 1))
        side = bands[:, :rows].reshape(width, owned, mine_cols)
        precond = jnp.einsum("kij,jkc->ikc", left_roots, side, preferred_element_type=f32)
        pre_sq = jnp.sum(precond * precond, axis=(0, 2))
        sums = jnp.concatenate([grad_sq, pre_sq])
        sums = jnp.broadcast_to(sums[:, None], (2 * owned, 128))
        sums = jnp.pad(sums, ((0, 8 - 2 * owned), (0, 0)))
        sums = jnp.sum(exchange(spread(sums, ng), group), axis=0)[: 2 * owned, 0]
        grad_sq, pre_sq = sums[:owned], sums[owned:]
        scale = jnp.sqrt(grad_sq / (pre_sq + epsilon))
        all_rows = jnp.arange(width, dtype=jnp.int32)
        c = jnp.arange(mine_cols, dtype=jnp.int32)
        own_cols = x * cols + (c // slab) * (slab * nzl) + zl * slab + c % slab
        mask = (all_rows[:, None, None] < bounds[:, 0][None, :, None]) & (
            own_cols[None, None, :] < bounds[:, 1][None, :, None]
        )
        step = jnp.where(mask, scale[None, :, None] * precond, 0.0)
        fresh = (base_cols - step_rate * step.reshape(width, owned * mine_cols)).astype(bf16)
        fresh = spread(fresh.reshape(nm, rows, owned * mine_cols), ng)
        back = exchange(fresh.reshape(ng * nm, rows, owned * mine_cols), wide)
        back = back.reshape(nx, nzl, nm, rows, owned * mine_cols)
        lane = jnp.arange(owned * mine_cols, dtype=jnp.int32)
        s_in, c_in = lane // mine_cols, lane % mine_cols
        to = s_in * cols + (c_in // slab) * (slab * nzl) + c_in % slab
        to = jnp.arange(nzl, dtype=jnp.int32)[:, None] * slab + to[None, :]
        place = (to[:, :, None] == jnp.arange(owned * cols, dtype=jnp.int32)).astype(bf16)
        spread_out = jnp.einsum(
            "xzmrl,zln->mrxn", back, place, preferred_element_type=f32
        ).astype(bf16)
        spread_out = spread_out.reshape(nm, rows, nx, owned, cols).transpose(0, 3, 1, 2, 4)
        weights = jnp.take(spread_out.reshape(blocks, rows, width), owner_slot, axis=0)

        own_step = lax.dynamic_slice_in_dim(step, zh * slab, slab, 2).transpose(1, 0, 2)
        new_momentum = beta_decay * momentum + own_step
        new_master = master - step_rate * new_momentum
        return (new_momentum, new_master, weights)

    return local


def solution(mesh):
    nm = mesh.shape["mp"]
    nzl, nzh = 2, nm
    nx = mesh.shape["dp"] // (nzl * nzh)
    fine = Mesh(mesh.devices.reshape(nx, nzh, nzl, nm), ("x", "zh", "zl", "mp"))
    dp = ("x", "zh", "zl")
    slab_spec = P("mp", None, dp)
    return jax.shard_map(
        make_local(nx, nzh, nzl, nm),
        mesh=fine,
        in_specs=(
            P(dp, None, "mp", None),
            P(),
            P(),
            P("mp", None, None),
            slab_spec,
            slab_spec,
            slab_spec,
        ),
        out_specs=(slab_spec, slab_spec, P(None, "mp", None)),
        check_vma=False,
    )
```

```python
import functools

import jax
import jax.numpy as jnp
from jax import lax
from jax.experimental import pallas as pl
from jax.experimental.pallas import tpu as pltpu
from jax.sharding import Mesh, PartitionSpec as P

epsilon = 1e-06
beta_decay = 0.9
step_rate = 0.5
f32 = jnp.float32
bf16 = jnp.bfloat16
in_vmem = pl.BlockSpec(memory_space=pltpu.VMEM)
in_smem = pl.BlockSpec(memory_space=pltpu.SMEM)
params = pltpu.CompilerParams(vmem_limit_bytes=24 * 2**20)


def exchange(value, axes):
    return lax.all_to_all(value, axes, split_axis=0, concat_axis=0, tiled=True)


def bounds_of(slot, owner_ref, extent_ref):
    height, width = jnp.int32(0), jnp.int32(0)
    for b in range(owner_ref.shape[0]):
        hit = owner_ref[b] == slot
        height = jnp.where(hit, extent_ref[b, 0], height)
        width = jnp.where(hit, extent_ref[b, 1], width)
    return height, width


def iota(shape, dim):
    return lax.broadcasted_iota(jnp.int32, shape, dim)


def send_kernel(nx, nm, owned, owner_ref, grads_ref, out_ref):
    blocks, rows, width = grads_ref.shape
    cols = width // nx
    for b in range(blocks):
        slot = owner_ref[b]
        owner, place = slot // owned, slot % owned
        for x in range(nx):
            out_ref[(x * owned + place) * nm + owner] = grads_ref[b, :, x * cols : (x + 1) * cols]


def grad_kernel(owned, owner_ref, extent_ref, pieces_ref, out_ref, sq_ref):
    _, rows, cols = pieces_ref.shape
    x, zh = lax.axis_index("x"), lax.axis_index("zh")
    zl, m = lax.axis_index("zl"), lax.axis_index("mp")
    height, width = bounds_of(m * owned + zl, owner_ref, extent_ref)
    total = pieces_ref[0]
    for i in range(1, pieces_ref.shape[0]):
        total = total + pieces_ref[i]
    ok = (zh * rows + iota((rows, cols), 0) < height) & (x * cols + iota((rows, cols), 1) < width)
    grad = jnp.where(ok, total, 0.0)
    sq_ref[...] = jnp.broadcast_to(jnp.sum(grad * grad, axis=0, keepdims=True), sq_ref.shape)
    low = grad.astype(bf16)
    for i in range(out_ref.shape[0]):
        out_ref[i] = low


def side_kernel(nx, owned, cols_ref, roots_ref, sq_ref, high_ref, low_ref, out_ref):
    nzh, height, lanes = out_ref.shape
    rows = cols_ref.shape[1]
    mine = roots_ref.shape[1]
    parts = []
    for s in range(owned):
        acc = jnp.zeros((rows, mine), f32)
        for x in range(nx):
            acc = acc + lax.dot_general(
                cols_ref[x * owned + s],
                roots_ref[s, :, x * lanes : (x + 1) * lanes],
                (((1,), (1,)), ((), ())),
                preferred_element_type=f32,
            )
        parts.append(acc)
    right = jnp.concatenate(parts, axis=1).astype(bf16)
    sq = sq_ref[...]
    first = sq.astype(bf16).astype(f32)
    second = (sq - first).astype(bf16).astype(f32)
    third = sq - first - second
    row = iota(sq.shape, 0)
    extra = jnp.where(row == 0, first, jnp.where(row == 1, second, jnp.where(row == 2, third, 0.0)))
    extra = jnp.concatenate([extra, jnp.zeros_like(extra)], axis=0).astype(bf16)
    for i in range(nzh):
        out_ref[i, :rows] = right
        out_ref[i, rows : rows + 16] = extra
        at = rows + 16
        for part_ref in (high_ref, low_ref):
            for x in range(nx):
                out_ref[i, at : at + 16] = part_ref[:, x * lanes : (x + 1) * lanes]
                at += 16


def left_kernel(nx, bands_ref, left_ref, precond_ref, base_ref, sums_ref, flip_ref):
    nzh, _, lanes = bands_ref.shape
    owned, width, _ = left_ref.shape
    rows = width // nzh
    mine = lanes // owned
    slab = mine // nzh
    side = bands_ref[:, :rows, :].reshape(width, lanes)
    lane = iota((width, lanes), 1)
    precond = jnp.zeros((width, lanes), f32)
    for s in range(owned):
        part = jnp.dot(left_ref[s], side, preferred_element_type=f32)
        precond = jnp.where(lane // mine == s, part, precond)
    precond_ref[...] = precond
    pre_sq = jnp.sum(precond * precond, axis=0, keepdims=True)
    extra = jnp.sum(bands_ref[:, rows : rows + 16, :].astype(f32), axis=0)
    grad_sq = jnp.sum(extra[:8], axis=0, keepdims=True)
    row = iota((8, lanes), 0)
    sums = jnp.where(row == 0, grad_sq, jnp.where(row == 1, pre_sq, 0.0))
    for i in range(sums_ref.shape[0]):
        sums_ref[i] = sums
    step = owned * slab
    for zh in range(nzh):
        for x in range(nx):
            at = rows + 16 + x * step
            value = bands_ref[zh, at : at + step, :].astype(f32)
            at = at + nx * step
            value = value + bands_ref[zh, at : at + step, :].astype(f32)
            for s in range(owned):
                flip_ref[s * mine + zh * slab : s * mine + (zh + 1) * slab, x * lanes : (x + 1) * lanes] = (
                    value[s * slab : (s + 1) * slab]
                )
    base_ref[...] = flip_ref[...].T


def fresh_kernel(
    nm, owned, slab, owner_ref, extent_ref, sums_ref, precond_ref, base_ref, out_ref, step_ref
):
    width, lanes = precond_ref.shape
    mine = lanes // owned
    ng = sums_ref.shape[0]
    nzl = owned
    x, zl, m = lax.axis_index("x"), lax.axis_index("zl"), lax.axis_index("mp")
    lane = iota((1, lanes), 1)
    place = lane // mine
    c = lane % mine
    column = x * lanes + (c // slab) * (slab * nzl) + zl * slab + c % slab
    scale = jnp.zeros((1, lanes), f32)
    height = jnp.zeros((1, lanes), jnp.int32)
    total = jnp.sum(sums_ref[...], axis=0)
    for s in range(owned):
        grad_rows = sums_ref[s]
        for g in range(s + nzl, ng, nzl):
            grad_rows = grad_rows + sums_ref[g]
        grad_sq = jnp.sum(grad_rows[0:1], axis=1, keepdims=True)
        pre_sq = jnp.sum(jnp.where(place == s, total[1:2], 0.0), axis=1, keepdims=True)
        tall, wide = bounds_of(m * owned + s, owner_ref, extent_ref)
        scale = jnp.where(place == s, jnp.sqrt(grad_sq / (pre_sq + epsilon)), scale)
        height = jnp.where(place == s, jnp.where(column < wide, tall, 0), height)
    rows = width // nm
    for i in range(nm):
        at = slice(i * rows, (i + 1) * rows)
        ok = i * rows + iota((rows, lanes), 0) < height
        step = jnp.where(ok, scale * precond_ref[at], 0.0)
        step_ref[at] = step
        fresh = (base_ref[at] - step_rate * step).astype(bf16)
        for g in range(ng):
            out_ref[g * nm + i] = fresh


def place_kernel(nx, nm, owned, owner_ref, back_ref, place_ref, out_ref):
    blocks, rows, width = out_ref.shape
    cols = width // nx
    for b in range(blocks):
        slot = owner_ref[b]
        owner, s = slot // owned, slot % owned
        lanes = []
        for zl in range(owned):
            lanes.append(
                jnp.concatenate([back_ref[(x * owned + zl) * nm + owner] for x in range(nx)], axis=0)
            )
        value = jnp.concatenate(lanes, axis=1)
        done = jnp.dot(value, place_ref[s], preferred_element_type=f32).astype(bf16)
        for x in range(nx):
            out_ref[b, :, x * cols : (x + 1) * cols] = done[x * rows : (x + 1) * rows]


def call(kernel, name, out, *args, scratch=()):
    specs = [in_smem if a.dtype == jnp.int32 else in_vmem for a in args]
    return pl.pallas_call(
        kernel,
        out_shape=out,
        in_specs=specs,
        out_specs=jax.tree.map(lambda _: in_vmem, out),
        scratch_shapes=list(scratch),
        compiler_params=params,
        name=name,
    )(*args)


def shape(dims, dtype):
    return jax.ShapeDtypeStruct(dims, dtype)


def make_local(nx, nzh, nzl, nm):
    ng = nx * nzl
    group = ("x", "zl")
    wide = ("x", "zl", "mp")

    def gather_along(value):
        zh = lax.axis_index("zh")
        held = value[None]
        stride = nzh // 2
        while stride:
            pairs = [(i, i ^ stride) for i in range(nzh)]
            other = lax.ppermute(held, "zh", pairs)
            first = (zh & stride) == 0
            low = jnp.where(first, held, other)
            high = jnp.where(first, other, held)
            held = jnp.stack([low, high], axis=1).reshape((-1,) + value.shape)
            stride //= 2
        return held

    def local(partial_grads, owner_slot, extent, left_roots, right_roots, momentum, master):
        blocks, rows, width = partial_grads.shape[1:]
        owned = left_roots.shape[0]
        slab = right_roots.shape[2]
        cols = width // nx
        mine_cols = slab * nzh
        lanes = owned * mine_cols
        zh = lax.axis_index("zh")

        roots = gather_along(jnp.swapaxes(right_roots, 1, 2))
        roots = jnp.swapaxes(roots, 0, 1).reshape(owned, mine_cols, width)
        base_t = jnp.swapaxes(master - (step_rate * beta_decay) * momentum, 1, 2)
        base_t = base_t.reshape(owned * slab, width)
        high = lax.reduce_precision(base_t, 8, 7)
        low = (base_t - high).astype(bf16)
        high = high.astype(bf16)

        send = call(
            functools.partial(send_kernel, nx, nm, owned),
            "blocks_to_owners",
            shape((ng * nm, rows, cols), bf16),
            owner_slot,
            partial_grads[0],
        )
        got = exchange(send, wide).reshape(ng, nm, rows, cols)
        part = got[0].astype(f32)
        for i in range(1, ng):
            part = part + got[i].astype(f32)
        pieces = exchange(part, "zh")
        grads, sq = call(
            functools.partial(grad_kernel, owned),
            "masked_grad",
            (shape((ng, rows, cols), bf16), shape((8, cols), f32)),
            owner_slot,
            extent,
            pieces,
        )
        all_cols = exchange(grads, group)
        packed = call(
            functools.partial(side_kernel, nx, owned),
            "right_side",
            shape((nzh, rows + 16 + 2 * nx * owned * slab, lanes), bf16),
            all_cols,
            roots,
            sq,
            high,
            low,
        )
        bands = exchange(packed, "zh")
        precond, base, sums = call(
            functools.partial(left_kernel, nx),
            "left_side",
            (shape((width, lanes), f32), shape((width, lanes), f32), shape((ng, 8, lanes), f32)),
            bands,
            left_roots,
            scratch=[pltpu.VMEM((lanes, width), f32)],
        )
        sums = exchange(sums, group)
        fresh, step = call(
            functools.partial(fresh_kernel, nm, owned, slab),
            "new_weights",
            (shape((ng * nm, rows, lanes), bf16), shape((width, lanes), f32)),
            owner_slot,
            extent,
            sums,
            precond,
            base,
        )
        back = exchange(fresh, wide)
        lane = jnp.arange(lanes, dtype=jnp.int32)
        c = lane % mine_cols
        to = jnp.arange(nzl, dtype=jnp.int32)[:, None] * slab + (c // slab) * (slab * nzl) + c % slab
        to = to.reshape(nzl * lanes)
        from_slot = jnp.tile(lane // mine_cols, nzl)
        place = (to[None, :, None] == jnp.arange(cols, dtype=jnp.int32)) & (
            from_slot[None, :, None] == jnp.arange(owned, dtype=jnp.int32)[:, None, None]
        )
        weights = call(
            functools.partial(place_kernel, nx, nm, owned),
            "blocks_in_order",
            shape((blocks, rows, width), bf16),
            owner_slot,
            back,
            place.astype(bf16),
        )

        step = step.reshape(width, owned, mine_cols)
        own_step = lax.dynamic_slice_in_dim(step, zh * slab, slab, 2).transpose(1, 0, 2)
        new_momentum = beta_decay * momentum + own_step
        new_master = master - step_rate * new_momentum
        return (new_momentum, new_master, weights)

    return local


def solution(mesh):
    nm = mesh.shape["mp"]
    nzl, nzh = 2, nm
    nx = mesh.shape["dp"] // (nzl * nzh)
    fine = Mesh(mesh.devices.reshape(nx, nzh, nzl, nm), ("x", "zh", "zl", "mp"))
    dp = ("x", "zh", "zl")
    slab_spec = P("mp", None, dp)
    return jax.shard_map(
        make_local(nx, nzh, nzl, nm),
        mesh=fine,
        in_specs=(
            P(dp, None, "mp", None),
            P(),
            P(),
            P("mp", None, None),
            slab_spec,
            slab_spec,
            slab_spec,
        ),
        out_specs=(slab_spec, slab_spec, P(None, "mp", None)),
        check_vma=False,
    )
```

```python
import functools

import jax
import jax.numpy as jnp
from jax import lax
from jax.experimental import pallas as pl
from jax.experimental.pallas import tpu as pltpu
from jax.sharding import Mesh, PartitionSpec as P

epsilon = 1e-06
beta_decay = 0.9
step_rate = 0.5
sum_unit = 2.0**11
base_unit = 2.0**12
f16 = jnp.float16
f32 = jnp.float32
bf16 = jnp.bfloat16
in_vmem = pl.BlockSpec(memory_space=pltpu.VMEM)
anywhere = pl.BlockSpec(memory_space=pl.ANY)
in_smem = pl.BlockSpec(memory_space=pltpu.SMEM)
params = pltpu.CompilerParams(vmem_limit_bytes=24 * 2**20)


def exchange(value, axes):
    return lax.all_to_all(value, axes, split_axis=0, concat_axis=0, tiled=True)


def spread(value, count):
    return jnp.broadcast_to(value[None], (count,) + value.shape)


def bounds_of(slot, owner_ref, extent_ref):
    height, width = jnp.int32(0), jnp.int32(0)
    for b in range(owner_ref.shape[0]):
        hit = owner_ref[b] == slot
        height = jnp.where(hit, extent_ref[b, 0], height)
        width = jnp.where(hit, extent_ref[b, 1], width)
    return height, width


def iota(shape, dim):
    return lax.broadcasted_iota(jnp.int32, shape, dim)


def send_kernel(nx, nm, owned, owner_ref, grads_ref, out_ref, sem):
    blocks, rows, width = grads_ref.shape
    cols = width // nx
    copies = []
    for b in range(blocks):
        slot = owner_ref[b]
        owner, place = slot // owned, slot % owned
        for x in range(nx):
            copy = pltpu.make_async_copy(
                grads_ref.at[b, :, x * cols : (x + 1) * cols],
                out_ref.at[(x * owned + place) * nm + owner],
                sem.at[b * nx + x],
            )
            copy.start()
            copies.append(copy)
    for copy in copies:
        copy.wait()


def grad_kernel(owned, owner_ref, extent_ref, pieces_ref, out_ref, sq_ref):
    _, rows, cols = pieces_ref.shape
    x, zh = lax.axis_index("x"), lax.axis_index("zh")
    zl, m = lax.axis_index("zl"), lax.axis_index("mp")
    height, width = bounds_of(m * owned + zl, owner_ref, extent_ref)
    total = pieces_ref[0]
    for i in range(1, pieces_ref.shape[0]):
        total = total + pieces_ref[i]
    ok = (zh * rows + iota((rows, cols), 0) < height) & (x * cols + iota((rows, cols), 1) < width)
    grad = jnp.where(ok, total, 0.0)
    sq_ref[...] = jnp.broadcast_to(jnp.sum(grad * grad, axis=0, keepdims=True), sq_ref.shape)
    low = grad.astype(bf16)
    for i in range(out_ref.shape[0]):
        out_ref[i] = low


def side_kernel(nx, owned, cols_ref, roots_ref, sq_ref, out_ref):
    nzh, height, lanes = out_ref.shape
    rows = cols_ref.shape[1]
    mine = roots_ref.shape[1]
    parts = []
    for s in range(owned):
        acc = jnp.zeros((rows, mine), f32)
        for x in range(nx):
            acc = acc + lax.dot_general(
                cols_ref[x * owned + s],
                roots_ref[s, :, x * lanes : (x + 1) * lanes],
                (((1,), (1,)), ((), ())),
                preferred_element_type=f32,
            )
        parts.append(acc)
    right = jnp.concatenate(parts, axis=1).astype(bf16)
    sq = sq_ref[...]
    first = sq.astype(bf16).astype(f32)
    second = (sq - first).astype(bf16).astype(f32)
    third = sq - first - second
    row = iota(sq.shape, 0)
    extra = jnp.where(row == 0, first, jnp.where(row == 1, second, jnp.where(row == 2, third, 0.0)))
    extra = jnp.concatenate([extra, jnp.zeros_like(extra)], axis=0).astype(bf16)
    for i in range(nzh):
        out_ref[i, :rows] = right
        out_ref[i, rows : rows + 16] = extra


def left_kernel(bands_ref, left_ref, base_t_ref, precond_ref, base_ref, sums_ref):
    nzh, _, lanes = bands_ref.shape
    owned, width, _ = left_ref.shape
    rows = width // nzh
    mine = lanes // owned
    side = bands_ref[:, :rows, :].reshape(width, lanes)
    lane = iota((width, lanes), 1)
    precond = jnp.zeros((width, lanes), f32)
    for s in range(owned):
        part = jnp.dot(left_ref[s], side, preferred_element_type=f32)
        precond = jnp.where(lane // mine == s, part, precond)
    precond_ref[...] = precond
    pre_sq = jnp.sum(precond * precond, axis=0, keepdims=True)
    extra = jnp.sum(bands_ref[:, rows : rows + 16, :].astype(f32), axis=0)
    grad_sq = jnp.sum(extra[:8], axis=0, keepdims=True)
    row = iota((8, lanes), 0)
    sums = jnp.where(row == 0, grad_sq, jnp.where(row == 1, pre_sq, 0.0))
    for i in range(sums_ref.shape[0]):
        sums_ref[i] = sums
    base_ref[...] = base_t_ref[...].T


def fresh_kernel(
    nm, owned, slab, owner_ref, extent_ref, sums_ref, precond_ref, base_ref, out_ref, step_ref, held_ref, sem
):
    width, lanes = precond_ref.shape
    mine = lanes // owned
    ng = sums_ref.shape[0]
    nzl = owned
    x, zl, m = lax.axis_index("x"), lax.axis_index("zl"), lax.axis_index("mp")
    lane = iota((1, lanes), 1)
    place = lane // mine
    c = lane % mine
    column = x * lanes + (c // slab) * (slab * nzl) + zl * slab + c % slab
    scale = jnp.zeros((1, lanes), f32)
    height = jnp.zeros((1, lanes), jnp.int32)
    total = jnp.sum(sums_ref[...], axis=0)
    for s in range(owned):
        grad_rows = sums_ref[s]
        for g in range(s + nzl, ng, nzl):
            grad_rows = grad_rows + sums_ref[g]
        grad_sq = jnp.sum(grad_rows[0:1], axis=1, keepdims=True)
        pre_sq = jnp.sum(jnp.where(place == s, total[1:2], 0.0), axis=1, keepdims=True)
        tall, wide = bounds_of(m * owned + s, owner_ref, extent_ref)
        scale = jnp.where(place == s, jnp.sqrt(grad_sq / (pre_sq + epsilon)), scale)
        height = jnp.where(place == s, jnp.where(column < wide, tall, 0), height)
    rows = width // nm
    for i in range(nm):
        at = slice(i * rows, (i + 1) * rows)
        ok = i * rows + iota((rows, lanes), 0) < height
        step = jnp.where(ok, scale * precond_ref[at], 0.0)
        step_ref[at] = step
        fresh = (base_ref[at] - step_rate * step).astype(bf16)
        held_ref[i] = fresh
    copies = []
    for g in range(ng):
        copy = pltpu.make_async_copy(held_ref, out_ref.at[g * nm : (g + 1) * nm], sem.at[g])
        copy.start()
        copies.append(copy)
    for copy in copies:
        copy.wait()


def place_kernel(nx, nm, owned, owner_ref, back_ref, place_ref, out_ref, held_ref, sem):
    blocks, rows, width = out_ref.shape
    cols = width // nx
    copies = []
    for b in range(blocks):
        slot = owner_ref[b]
        owner, s = slot // owned, slot % owned
        lanes = []
        for zl in range(owned):
            lanes.append(
                jnp.concatenate([back_ref[(x * owned + zl) * nm + owner] for x in range(nx)], axis=0)
            )
        value = jnp.concatenate(lanes, axis=1)
        done = jnp.dot(value, place_ref[s], preferred_element_type=f32).astype(bf16)
        for x in range(nx):
            held_ref[b, :, x * cols : (x + 1) * cols] = done[x * rows : (x + 1) * rows]
        copy = pltpu.make_async_copy(held_ref.at[b], out_ref.at[b], sem.at[b])
        copy.start()
        copies.append(copy)
    for copy in copies:
        copy.wait()


def call(kernel, name, out, *args, scratch=(), far=(), far_out=()):
    specs = [in_smem if a.dtype == jnp.int32 else in_vmem for a in args]
    for i in far:
        specs[i] = anywhere
    return pl.pallas_call(
        kernel,
        out_shape=out,
        in_specs=specs,
        out_specs=[anywhere if i in far_out else in_vmem for i in range(len(out))],
        scratch_shapes=list(scratch),
        compiler_params=params,
        name=name,
    )(*args)


def shape(dims, dtype):
    return jax.ShapeDtypeStruct(dims, dtype)


def make_local(nx, nzh, nzl, nm):
    ng = nx * nzl
    group = ("x", "zl")
    wide = ("x", "zl", "mp")

    def to_rows(value):
        owned, slab, width = value.shape
        value = value.reshape(owned * slab, nx, width // nx)
        return jnp.swapaxes(value, 0, 1).reshape(nx * owned * slab, width // nx)

    def from_rows(value, owned):
        count, height, cols = value.shape
        slab = height // (nx * owned)
        value = value.reshape(count, nx, owned, slab, cols).transpose(2, 0, 3, 1, 4)
        return value.reshape(owned * count * slab, nx * cols)

    def swap(held, stride):
        pairs = [(i, i ^ stride) for i in range(nzh)]
        other = lax.ppermute(held, "zh", pairs)
        first = (lax.axis_index("zh") & stride) == 0
        low = jnp.where(first, held, other)
        high = jnp.where(first, other, held)
        return jnp.stack([low, high], axis=1).reshape((-1,) + held.shape[1:])

    def local(partial_grads, owner_slot, extent, left_roots, right_roots, momentum, master):
        blocks, rows, width = partial_grads.shape[1:]
        owned = left_roots.shape[0]
        slab = right_roots.shape[2]
        cols = width // nx
        mine_cols = slab * nzh
        lanes = owned * mine_cols
        zh = lax.axis_index("zh")

        roots = jnp.swapaxes(right_roots, 1, 2)[None]
        strides = [nzh >> i for i in range(1, nzh.bit_length())]
        base_t = jnp.swapaxes(master - (step_rate * beta_decay) * momentum, 1, 2)
        (send,) = call(
            functools.partial(send_kernel, nx, nm, owned),
            "blocks_to_owners",
            [shape((ng * nm, rows, cols), bf16)],
            owner_slot,
            partial_grads[0],
            scratch=[pltpu.SemaphoreType.DMA((blocks * nx,))],
            far=(1,),
            far_out=(0,),
        )
        roots, send = lax.optimization_barrier((roots, send))
        roots = swap(roots, strides[0])
        got = exchange(send, wide).reshape(ng, nm, rows, cols)
        part = got[0].astype(f32)
        for i in range(1, ng):
            part = part + got[i].astype(f32)
        part = (part * sum_unit).astype(f16)
        base_rows = to_rows((base_t * base_unit).astype(f16))
        packed = jnp.concatenate([part, spread(base_rows, nzh)], axis=1)
        roots, packed = lax.optimization_barrier((roots, packed))
        for stride in strides[1:]:
            roots = swap(roots, stride)
        roots = jnp.swapaxes(roots, 0, 1).reshape(owned, mine_cols, width)
        pieces = exchange(packed, "zh")
        base_t = from_rows(pieces[:, rows:], owned).astype(f32) * (1.0 / base_unit)
        pieces = pieces[:, :rows].astype(f32) * (1.0 / sum_unit)
        grads, sq = call(
            functools.partial(grad_kernel, owned),
            "masked_grad",
            (shape((ng, rows, cols), bf16), shape((8, cols), f32)),
            owner_slot,
            extent,
            pieces,
        )
        all_cols = exchange(grads, group)
        (packed,) = call(
            functools.partial(side_kernel, nx, owned),
            "right_side",
            [shape((nzh, rows + 16, lanes), bf16)],
            all_cols,
            roots,
            sq,
        )
        bands = exchange(packed, "zh")
        precond, base, sums = call(
            left_kernel,
            "left_side",
            (shape((width, lanes), f32), shape((width, lanes), f32), shape((ng, 8, lanes), f32)),
            bands,
            left_roots,
            base_t,
        )
        sums = exchange(sums, group)
        fresh, step = call(
            functools.partial(fresh_kernel, nm, owned, slab),
            "new_weights",
            (shape((ng * nm, rows, lanes), bf16), shape((width, lanes), f32)),
            owner_slot,
            extent,
            sums,
            precond,
            base,
            scratch=[pltpu.VMEM((nm, rows, lanes), bf16), pltpu.SemaphoreType.DMA((ng,))],
            far_out=(0,),
        )
        back = exchange(fresh, wide)
        lane = jnp.arange(lanes, dtype=jnp.int32)
        c = lane % mine_cols
        to = jnp.arange(nzl, dtype=jnp.int32)[:, None] * slab + (c // slab) * (slab * nzl) + c % slab
        to = to.reshape(nzl * lanes)
        from_slot = jnp.tile(lane // mine_cols, nzl)
        place = (to[None, :, None] == jnp.arange(cols, dtype=jnp.int32)) & (
            from_slot[None, :, None] == jnp.arange(owned, dtype=jnp.int32)[:, None, None]
        )
        (weights,) = call(
            functools.partial(place_kernel, nx, nm, owned),
            "blocks_in_order",
            [shape((blocks, rows, width), bf16)],
            owner_slot,
            back,
            place.astype(bf16),
            scratch=[pltpu.VMEM((blocks, rows, width), bf16), pltpu.SemaphoreType.DMA((blocks,))],
            far_out=(0,),
        )

        step = step.reshape(width, owned, mine_cols)
        own_step = lax.dynamic_slice_in_dim(step, zh * slab, slab, 2).transpose(1, 0, 2)
        new_momentum = beta_decay * momentum + own_step
        new_master = master - step_rate * new_momentum
        return (new_momentum, new_master, weights)

    return local


def solution(mesh):
    nm = mesh.shape["mp"]
    nzl, nzh = 2, nm
    nx = mesh.shape["dp"] // (nzl * nzh)
    fine = Mesh(mesh.devices.reshape(nx, nzh, nzl, nm), ("x", "zh", "zl", "mp"))
    dp = ("x", "zh", "zl")
    slab_spec = P("mp", None, dp)
    return jax.shard_map(
        make_local(nx, nzh, nzl, nm),
        mesh=fine,
        in_specs=(
            P(dp, None, "mp", None),
            P(),
            P(),
            P("mp", None, None),
            slab_spec,
            slab_spec,
            slab_spec,
        ),
        out_specs=(slab_spec, slab_spec, P(None, "mp", None)),
        check_vma=False,
    )
```

```python
import functools

import jax
import jax.numpy as jnp
from jax import lax
from jax.experimental import pallas as pl
from jax.experimental.pallas import tpu as pltpu
from jax.sharding import Mesh, PartitionSpec as P

epsilon = 1e-06
beta_decay = 0.9
step_rate = 0.5
sum_unit = 2.0**11
base_unit = 2.0**12
f16 = jnp.float16
f32 = jnp.float32
bf16 = jnp.bfloat16
in_vmem = pl.BlockSpec(memory_space=pltpu.VMEM)
in_hbm = pl.BlockSpec(memory_space=pltpu.HBM)
in_smem = pl.BlockSpec(memory_space=pltpu.SMEM)


def exchange(value, axes):
    return lax.all_to_all(value, axes, split_axis=0, concat_axis=0, tiled=True)


def spread(value, count):
    return jnp.broadcast_to(value[None], (count,) + value.shape)


def bounds_of(slot, meta_ref):
    height, width = jnp.int32(0), jnp.int32(0)
    blocks = meta_ref.shape[0] // 3
    for b in range(blocks):
        hit = meta_ref[b] == slot
        height = jnp.where(hit, meta_ref[blocks + b], height)
        width = jnp.where(hit, meta_ref[2 * blocks + b], width)
    return height, width


def iota(shape, dim):
    return lax.broadcasted_iota(jnp.int32, shape, dim)


def send_kernel(
    nx, nm, owned, slots_ref, grads_ref, out_ref, owner_ref, held_ref, sem_slots, sem_in, sem_out
):
    blocks, rows, width = grads_ref.shape
    cols = width // nx
    slots = pltpu.make_async_copy(slots_ref, owner_ref, sem_slots)
    slots.start()
    reads = []
    for b in range(blocks):
        read = pltpu.make_async_copy(grads_ref.at[b], held_ref.at[b], sem_in.at[b])
        read.start()
        reads.append(read)
    slots.wait()
    copies = []
    for b in range(blocks):
        slot = owner_ref[b]
        owner, place = slot // owned, slot % owned
        reads[b].wait()
        for x in range(nx):
            copy = pltpu.make_async_copy(
                held_ref.at[b, :, x * cols : (x + 1) * cols],
                out_ref.at[(x * owned + place) * nm + owner],
                sem_out.at[b * nx + x],
            )
            copy.start()
            copies.append(copy)
    for copy in copies:
        copy.wait()


def grad_kernel(owned, meta_ref, pieces_ref, out_ref, sq_ref):
    _, rows, cols = pieces_ref.shape
    x, zh = lax.axis_index("x"), lax.axis_index("zh")
    zl, m = lax.axis_index("zl"), lax.axis_index("mp")
    height, width = bounds_of(m * owned + zl, meta_ref)
    total = pieces_ref[0]
    for i in range(1, pieces_ref.shape[0]):
        total = total + pieces_ref[i]
    ok = (zh * rows + iota((rows, cols), 0) < height) & (x * cols + iota((rows, cols), 1) < width)
    grad = jnp.where(ok, total, 0.0)
    sq_ref[...] = jnp.broadcast_to(jnp.sum(grad * grad, axis=0, keepdims=True), sq_ref.shape)
    low = grad.astype(bf16)
    for i in range(out_ref.shape[0]):
        out_ref[i] = low


def side_kernel(nx, owned, cols_ref, roots_ref, sq_ref, out_ref):
    nzh, height, lanes = out_ref.shape
    rows = cols_ref.shape[1]
    mine = roots_ref.shape[1]
    parts = []
    for s in range(owned):
        acc = jnp.zeros((rows, mine), f32)
        for x in range(nx):
            acc = acc + lax.dot_general(
                cols_ref[x * owned + s],
                roots_ref[s, :, x * lanes : (x + 1) * lanes],
                (((1,), (1,)), ((), ())),
                preferred_element_type=f32,
            )
        parts.append(acc)
    right = jnp.concatenate(parts, axis=1).astype(bf16)
    sq = sq_ref[...]
    first = sq.astype(bf16).astype(f32)
    second = (sq - first).astype(bf16).astype(f32)
    third = sq - first - second
    row = iota(sq.shape, 0)
    extra = jnp.where(row == 0, first, jnp.where(row == 1, second, jnp.where(row == 2, third, 0.0)))
    extra = jnp.concatenate([extra, jnp.zeros_like(extra)], axis=0).astype(bf16)
    for i in range(nzh):
        out_ref[i, :rows] = right
        out_ref[i, rows : rows + 16] = extra


def left_kernel(bands_ref, left_ref, base_t_ref, precond_ref, base_ref, sums_ref):
    nzh, _, lanes = bands_ref.shape
    owned, width, _ = left_ref.shape
    rows = width // nzh
    mine = lanes // owned
    side = bands_ref[:, :rows, :].reshape(width, lanes)
    lane = iota((width, lanes), 1)
    precond = jnp.zeros((width, lanes), f32)
    for s in range(owned):
        part = jnp.dot(left_ref[s], side, preferred_element_type=f32)
        precond = jnp.where(lane // mine == s, part, precond)
    precond_ref[...] = precond
    pre_sq = jnp.sum(precond * precond, axis=0, keepdims=True)
    extra = jnp.sum(bands_ref[:, rows : rows + 16, :].astype(f32), axis=0)
    grad_sq = jnp.sum(extra[:8], axis=0, keepdims=True)
    row = iota((8, lanes), 0)
    sums = jnp.where(row == 0, grad_sq, jnp.where(row == 1, pre_sq, 0.0))
    for i in range(sums_ref.shape[0]):
        sums_ref[i] = sums
    base_ref[...] = base_t_ref[...].T


def fresh_kernel(
    nm, owned, slab, meta_ref, sums_ref, precond_ref, base_ref, out_ref, step_ref, held_ref, sem
):
    width, lanes = precond_ref.shape
    mine = lanes // owned
    ng = sums_ref.shape[0]
    nzl = owned
    x, zl, m = lax.axis_index("x"), lax.axis_index("zl"), lax.axis_index("mp")
    lane = iota((1, lanes), 1)
    place = lane // mine
    c = lane % mine
    column = x * lanes + (c // slab) * (slab * nzl) + zl * slab + c % slab
    scale = jnp.zeros((1, lanes), f32)
    height = jnp.zeros((1, lanes), jnp.int32)
    total = jnp.sum(sums_ref[...], axis=0)
    for s in range(owned):
        grad_rows = sums_ref[s]
        for g in range(s + nzl, ng, nzl):
            grad_rows = grad_rows + sums_ref[g]
        grad_sq = jnp.sum(grad_rows[0:1], axis=1, keepdims=True)
        pre_sq = jnp.sum(jnp.where(place == s, total[1:2], 0.0), axis=1, keepdims=True)
        tall, wide = bounds_of(m * owned + s, meta_ref)
        scale = jnp.where(place == s, jnp.sqrt(grad_sq / (pre_sq + epsilon)), scale)
        height = jnp.where(place == s, jnp.where(column < wide, tall, 0), height)
    rows = width // nm
    copies = []
    for i in range(nm):
        at = slice(i * rows, (i + 1) * rows)
        ok = i * rows + iota((rows, lanes), 0) < height
        step = jnp.where(ok, scale * precond_ref[at], 0.0)
        step_ref[at] = step
        fresh = (base_ref[at] - step_rate * step).astype(bf16)
        held_ref[i] = fresh
        if i % 2 == 0:
            continue
        for g in range(ng):
            copy = pltpu.make_async_copy(
                held_ref.at[i - 1 : i + 1],
                out_ref.at[g * nm + i - 1 : g * nm + i + 1],
                sem.at[i // 2 * ng + g],
            )
            copy.start()
            copies.append(copy)
    for copy in copies:
        copy.wait()


def place_kernel(nx, nm, owned, meta_ref, back_ref, place_ref, out_ref, held_ref, sem):
    blocks, rows, width = out_ref.shape
    cols = width // nx
    copies = []
    for b in range(blocks):
        slot = meta_ref[b]
        owner, s = slot // owned, slot % owned
        lanes = []
        for zl in range(owned):
            lanes.append(
                jnp.concatenate([back_ref[(x * owned + zl) * nm + owner] for x in range(nx)], axis=0)
            )
        value = jnp.concatenate(lanes, axis=1)
        done = jnp.dot(value, place_ref[s], preferred_element_type=f32).astype(bf16)
        for x in range(nx):
            held_ref[b, :, x * cols : (x + 1) * cols] = done[x * rows : (x + 1) * rows]
        copy = pltpu.make_async_copy(held_ref.at[b], out_ref.at[b], sem.at[b])
        copy.start()
        copies.append(copy)
    for copy in copies:
        copy.wait()


def call(kernel, name, out, *args, scratch=(), far=(), far_out=(), vmem=24):
    specs = [in_smem if a.dtype == jnp.int32 else in_vmem for a in args]
    for i in far:
        specs[i] = in_hbm
    return pl.pallas_call(
        kernel,
        out_shape=out,
        in_specs=specs,
        out_specs=[in_hbm if i in far_out else in_vmem for i in range(len(out))],
        scratch_shapes=list(scratch),
        compiler_params=pltpu.CompilerParams(vmem_limit_bytes=vmem * 2**20),
        name=name,
    )(*args)


def shape(dims, dtype):
    return jax.ShapeDtypeStruct(dims, dtype)


def make_local(nx, nzh, nzl, nm):
    ng = nx * nzl
    group = ("x", "zl")
    wide = ("x", "zl", "mp")

    def to_rows(value):
        owned, slab, width = value.shape
        value = value.reshape(owned * slab, nx, width // nx)
        return jnp.swapaxes(value, 0, 1).reshape(nx * owned * slab, width // nx)

    def from_rows(value, owned):
        count, height, cols = value.shape
        slab = height // (nx * owned)
        value = value.reshape(count, nx, owned, slab, cols).transpose(2, 0, 3, 1, 4)
        return value.reshape(owned * count * slab, nx * cols)

    def swap(held, stride):
        pairs = [(i, i ^ stride) for i in range(nzh)]
        other = lax.ppermute(held, "zh", pairs)
        first = (lax.axis_index("zh") & stride) == 0
        low = jnp.where(first, held, other)
        high = jnp.where(first, other, held)
        return jnp.stack([low, high], axis=1).reshape((-1,) + held.shape[1:])

    def local(partial_grads, owner_slot, extent, left_roots, right_roots, momentum, master):
        blocks, rows, width = partial_grads.shape[1:]
        owned = left_roots.shape[0]
        slab = right_roots.shape[2]
        cols = width // nx
        mine_cols = slab * nzh
        lanes = owned * mine_cols
        zh = lax.axis_index("zh")

        roots = jnp.swapaxes(right_roots, 1, 2)[None]
        strides = [nzh >> i for i in range(1, nzh.bit_length())]
        base_t = jnp.swapaxes(master - (step_rate * beta_decay) * momentum, 1, 2)
        (send,) = call(
            functools.partial(send_kernel, nx, nm, owned),
            "blocks_to_owners",
            [shape((ng * nm, rows, cols), bf16)],
            owner_slot,
            partial_grads[0],
            scratch=[
                pltpu.SMEM((blocks,), jnp.int32),
                pltpu.VMEM((blocks, rows, width), bf16),
                pltpu.SemaphoreType.DMA,
                pltpu.SemaphoreType.DMA((blocks,)),
                pltpu.SemaphoreType.DMA((blocks * nx,)),
            ],
            far=(0, 1),
            far_out=(0,),
            vmem=60,
        )
        roots, send = lax.optimization_barrier((roots, send))
        roots = swap(roots, strides[0])
        got = exchange(send, wide).reshape(ng, nm, rows, cols)
        part = got[0].astype(f32)
        for i in range(1, ng):
            part = part + got[i].astype(f32)
        part = (part * sum_unit).astype(f16)
        base_rows = to_rows((base_t * base_unit).astype(f16))
        packed = jnp.concatenate([part, spread(base_rows, nzh)], axis=1)
        meta = jnp.concatenate([owner_slot, extent[:, 0], extent[:, 1]])
        meta, roots, packed = lax.optimization_barrier((meta, roots, packed))
        for stride in strides[1:]:
            roots = swap(roots, stride)
        roots = jnp.swapaxes(roots, 0, 1).reshape(owned, mine_cols, width)
        pieces = exchange(packed, "zh")
        base_t = from_rows(pieces[:, rows:], owned).astype(f32) * (1.0 / base_unit)
        pieces = pieces[:, :rows].astype(f32) * (1.0 / sum_unit)
        grads, sq = call(
            functools.partial(grad_kernel, owned),
            "masked_grad",
            (shape((ng, rows, cols), bf16), shape((8, cols), f32)),
            meta,
            pieces,
        )
        all_cols = exchange(grads, group)
        (packed,) = call(
            functools.partial(side_kernel, nx, owned),
            "right_side",
            [shape((nzh, rows + 16, lanes), bf16)],
            all_cols,
            roots,
            sq,
        )
        bands = exchange(packed, "zh")
        precond, base, sums = call(
            left_kernel,
            "left_side",
            (shape((width, lanes), f32), shape((width, lanes), f32), shape((ng, 8, lanes), f32)),
            bands,
            left_roots,
            base_t,
        )
        sums = exchange(sums, group)
        fresh, step = call(
            functools.partial(fresh_kernel, nm, owned, slab),
            "new_weights",
            (shape((ng * nm, rows, lanes), bf16), shape((width, lanes), f32)),
            meta,
            sums,
            precond,
            base,
            scratch=[pltpu.VMEM((nm, rows, lanes), bf16), pltpu.SemaphoreType.DMA((nm // 2 * ng,))],
            far_out=(0,),
        )
        back = exchange(fresh, wide)
        lane = jnp.arange(lanes, dtype=jnp.int32)
        c = lane % mine_cols
        to = jnp.arange(nzl, dtype=jnp.int32)[:, None] * slab + (c // slab) * (slab * nzl) + c % slab
        to = to.reshape(nzl * lanes)
        from_slot = jnp.tile(lane // mine_cols, nzl)
        place = (to[None, :, None] == jnp.arange(cols, dtype=jnp.int32)) & (
            from_slot[None, :, None] == jnp.arange(owned, dtype=jnp.int32)[:, None, None]
        )
        (weights,) = call(
            functools.partial(place_kernel, nx, nm, owned),
            "blocks_in_order",
            [shape((blocks, rows, width), bf16)],
            meta,
            back,
            place.astype(bf16),
            scratch=[pltpu.VMEM((blocks, rows, width), bf16), pltpu.SemaphoreType.DMA((blocks,))],
            far_out=(0,),
        )

        step = step.reshape(width, owned, mine_cols)
        own_step = lax.dynamic_slice_in_dim(step, zh * slab, slab, 2).transpose(1, 0, 2)
        new_momentum = beta_decay * momentum + own_step
        new_master = master - step_rate * new_momentum
        return (new_momentum, new_master, weights)

    return local


def solution(mesh):
    nm = mesh.shape["mp"]
    nzl, nzh = 2, nm
    nx = mesh.shape["dp"] // (nzl * nzh)
    fine = Mesh(mesh.devices.reshape(nx, nzh, nzl, nm), ("x", "zh", "zl", "mp"))
    dp = ("x", "zh", "zl")
    slab_spec = P("mp", None, dp)
    return jax.shard_map(
        make_local(nx, nzh, nzl, nm),
        mesh=fine,
        in_specs=(
            P(dp, None, "mp", None),
            P(),
            P(),
            P("mp", None, None),
            slab_spec,
            slab_spec,
            slab_spec,
        ),
        out_specs=(slab_spec, slab_spec, P(None, "mp", None)),
        check_vma=False,
    )
```

```python
import functools

import jax
import jax.numpy as jnp
from jax import lax
from jax.experimental import pallas as pl
from jax.experimental.pallas import tpu as pltpu
from jax.sharding import Mesh, PartitionSpec as P

epsilon = 1e-06
beta_decay = 0.9
step_rate = 0.5
sum_unit = 2.0**11
base_unit = 2.0**12
f16 = jnp.float16
f32 = jnp.float32
bf16 = jnp.bfloat16
in_vmem = pl.BlockSpec(memory_space=pltpu.VMEM)
in_hbm = pl.BlockSpec(memory_space=pltpu.HBM)
in_smem = pl.BlockSpec(memory_space=pltpu.SMEM)


def exchange(value, axes):
    return lax.all_to_all(value, axes, split_axis=0, concat_axis=0, tiled=True)


def spread(value, count):
    return jnp.broadcast_to(value[None], (count,) + value.shape)


def bounds_of(slot, meta_ref):
    height, width = jnp.int32(0), jnp.int32(0)
    blocks = meta_ref.shape[0] // 3
    for b in range(blocks):
        hit = meta_ref[b] == slot
        height = jnp.where(hit, meta_ref[blocks + b], height)
        width = jnp.where(hit, meta_ref[2 * blocks + b], width)
    return height, width


def iota(shape, dim):
    return lax.broadcasted_iota(jnp.int32, shape, dim)


def send_kernel(
    nx, nm, owned, slots_ref, grads_ref, out_ref, owner_ref, held_ref, sem_slots, sem_in, sem_out
):
    blocks, rows, width = grads_ref.shape
    cols = width // nx
    slots = pltpu.make_async_copy(slots_ref, owner_ref, sem_slots)
    slots.start()
    reads = []
    for b in range(blocks):
        read = pltpu.make_async_copy(grads_ref.at[b], held_ref.at[b], sem_in.at[b])
        read.start()
        reads.append(read)
    slots.wait()
    copies = []
    for b in range(blocks):
        slot = owner_ref[b]
        owner, place = slot // owned, slot % owned
        reads[b].wait()
        for x in range(nx):
            copy = pltpu.make_async_copy(
                held_ref.at[b, :, x * cols : (x + 1) * cols],
                out_ref.at[(x * owned + place) * nm + owner],
                sem_out.at[b * nx + x],
            )
            copy.start()
            copies.append(copy)
    for copy in copies:
        copy.wait()


def grad_kernel(owned, meta_ref, pieces_ref, out_ref, sq_ref):
    _, rows, cols = pieces_ref.shape
    x, zh = lax.axis_index("x"), lax.axis_index("zh")
    zl, m = lax.axis_index("zl"), lax.axis_index("mp")
    height, width = bounds_of(m * owned + zl, meta_ref)
    total = pieces_ref[0]
    for i in range(1, pieces_ref.shape[0]):
        total = total + pieces_ref[i]
    ok = (zh * rows + iota((rows, cols), 0) < height) & (x * cols + iota((rows, cols), 1) < width)
    grad = jnp.where(ok, total, 0.0)
    sq_ref[...] = jnp.broadcast_to(jnp.sum(grad * grad, axis=0, keepdims=True), sq_ref.shape)
    low = grad.astype(bf16)
    for i in range(out_ref.shape[0]):
        out_ref[i] = low


def side_kernel(nx, owned, cols_ref, roots_ref, sq_ref, out_ref):
    nzh, height, lanes = out_ref.shape
    rows = cols_ref.shape[1]
    mine = roots_ref.shape[1]
    parts = []
    for s in range(owned):
        acc = jnp.zeros((rows, mine), f32)
        for x in range(nx):
            acc = acc + lax.dot_general(
                cols_ref[x * owned + s],
                roots_ref[s, :, x * lanes : (x + 1) * lanes],
                (((1,), (1,)), ((), ())),
                preferred_element_type=f32,
            )
        parts.append(acc)
    right = jnp.concatenate(parts, axis=1).astype(bf16)
    sq = sq_ref[...]
    first = sq.astype(bf16).astype(f32)
    second = (sq - first).astype(bf16).astype(f32)
    third = sq - first - second
    row = iota(sq.shape, 0)
    extra = jnp.where(row == 0, first, jnp.where(row == 1, second, jnp.where(row == 2, third, 0.0)))
    extra = jnp.concatenate([extra, jnp.zeros_like(extra)], axis=0).astype(bf16)
    for i in range(nzh):
        out_ref[i, :rows] = right
        out_ref[i, rows : rows + 16] = extra


def left_kernel(bands_ref, left_ref, base_t_ref, precond_ref, base_ref, sums_ref):
    nzh, _, lanes = bands_ref.shape
    owned, width, _ = left_ref.shape
    rows = width // nzh
    mine = lanes // owned
    side = bands_ref[:, :rows, :].reshape(width, lanes)
    lane = iota((width, lanes), 1)
    precond = jnp.zeros((width, lanes), f32)
    for s in range(owned):
        part = jnp.dot(left_ref[s], side, preferred_element_type=f32)
        precond = jnp.where(lane // mine == s, part, precond)
    precond_ref[...] = precond
    pre_sq = jnp.sum(precond * precond, axis=0, keepdims=True)
    extra = jnp.sum(bands_ref[:, rows : rows + 16, :].astype(f32), axis=0)
    grad_sq = jnp.sum(extra[:8], axis=0, keepdims=True)
    row = iota((8, lanes), 0)
    sums = jnp.where(row == 0, grad_sq, jnp.where(row == 1, pre_sq, 0.0))
    for i in range(sums_ref.shape[0]):
        sums_ref[i] = sums
    base_ref[...] = base_t_ref[...].T


def fresh_kernel(
    nm, owned, slab, meta_ref, sums_ref, precond_ref, base_ref, out_ref, step_ref, held_ref, sem
):
    width, lanes = precond_ref.shape
    mine = lanes // owned
    ng = sums_ref.shape[0]
    nzl = owned
    x, zl, m = lax.axis_index("x"), lax.axis_index("zl"), lax.axis_index("mp")
    lane = iota((1, lanes), 1)
    place = lane // mine
    c = lane % mine
    column = x * lanes + (c // slab) * (slab * nzl) + zl * slab + c % slab
    scale = jnp.zeros((1, lanes), f32)
    height = jnp.zeros((1, lanes), jnp.int32)
    total = jnp.sum(sums_ref[...], axis=0)
    for s in range(owned):
        grad_rows = sums_ref[s]
        for g in range(s + nzl, ng, nzl):
            grad_rows = grad_rows + sums_ref[g]
        grad_sq = jnp.sum(grad_rows[0:1], axis=1, keepdims=True)
        pre_sq = jnp.sum(jnp.where(place == s, total[1:2], 0.0), axis=1, keepdims=True)
        tall, wide = bounds_of(m * owned + s, meta_ref)
        scale = jnp.where(place == s, jnp.sqrt(grad_sq / (pre_sq + epsilon)), scale)
        height = jnp.where(place == s, jnp.where(column < wide, tall, 0), height)
    rows = width // nm
    copies = []
    for i in range(nm):
        at = slice(i * rows, (i + 1) * rows)
        ok = i * rows + iota((rows, lanes), 0) < height
        step = jnp.where(ok, scale * precond_ref[at], 0.0)
        step_ref[at] = step
        fresh = (base_ref[at] - step_rate * step).astype(bf16)
        held_ref[i] = fresh
        if i % 2 == 0:
            continue
        for g in range(ng):
            copy = pltpu.make_async_copy(
                held_ref.at[i - 1 : i + 1],
                out_ref.at[g * nm + i - 1 : g * nm + i + 1],
                sem.at[i // 2 * ng + g],
            )
            copy.start()
            copies.append(copy)
    for copy in copies:
        copy.wait()


def place_kernel(nx, nm, owned, meta_ref, back_ref, place_ref, out_ref, held_ref, sem):
    blocks, rows, width = out_ref.shape
    cols = width // nx
    copies = []
    for b in range(blocks):
        slot = meta_ref[b]
        owner, s = slot // owned, slot % owned
        lanes = []
        for zl in range(owned):
            lanes.append(
                jnp.concatenate([back_ref[(x * owned + zl) * nm + owner] for x in range(nx)], axis=0)
            )
        value = jnp.concatenate(lanes, axis=1)
        done = jnp.dot(value, place_ref[s], preferred_element_type=f32).astype(bf16)
        for x in range(nx):
            held_ref[b, :, x * cols : (x + 1) * cols] = done[x * rows : (x + 1) * rows]
        copy = pltpu.make_async_copy(held_ref.at[b], out_ref.at[b], sem.at[b])
        copy.start()
        copies.append(copy)
    for copy in copies:
        copy.wait()


def call(kernel, name, out, *args, scratch=(), far=(), far_out=(), vmem=24):
    specs = [in_smem if a.dtype == jnp.int32 else in_vmem for a in args]
    for i in far:
        specs[i] = in_hbm
    return pl.pallas_call(
        kernel,
        out_shape=out,
        in_specs=specs,
        out_specs=[in_hbm if i in far_out else in_vmem for i in range(len(out))],
        scratch_shapes=list(scratch),
        compiler_params=pltpu.CompilerParams(vmem_limit_bytes=vmem * 2**20),
        name=name,
    )(*args)


def shape(dims, dtype):
    return jax.ShapeDtypeStruct(dims, dtype)


def make_local(nx, nzh, nzl, nm):
    ng = nx * nzl
    group = ("x", "zl")
    wide = ("x", "zl", "mp")

    def to_rows(value):
        owned, slab, width = value.shape
        value = value.reshape(owned * slab, nx, width // nx)
        return jnp.swapaxes(value, 0, 1).reshape(nx * owned * slab, width // nx)

    def from_rows(value, owned):
        count, height, cols = value.shape
        slab = height // (nx * owned)
        value = value.reshape(count, nx, owned, slab, cols).transpose(2, 0, 3, 1, 4)
        return value.reshape(owned * count * slab, nx * cols)

    def swap(held, stride):
        pairs = [(i, i ^ stride) for i in range(nzh)]
        other = lax.ppermute(held, "zh", pairs)
        first = (lax.axis_index("zh") & stride) == 0
        low = jnp.where(first, held, other)
        high = jnp.where(first, other, held)
        return jnp.stack([low, high], axis=1).reshape((-1,) + held.shape[1:])

    def local(partial_grads, owner_slot, extent, left_roots, right_roots, momentum, master):
        blocks, rows, width = partial_grads.shape[1:]
        owned = left_roots.shape[0]
        slab = right_roots.shape[2]
        cols = width // nx
        mine_cols = slab * nzh
        lanes = owned * mine_cols
        zh = lax.axis_index("zh")

        roots = jnp.swapaxes(right_roots, 1, 2)[None]
        strides = [nzh >> i for i in range(1, nzh.bit_length())]
        base_t = jnp.swapaxes(master - (step_rate * beta_decay) * momentum, 1, 2)
        (send,) = call(
            functools.partial(send_kernel, nx, nm, owned),
            "blocks_to_owners",
            [shape((ng * nm, rows, cols), bf16)],
            owner_slot,
            partial_grads[0],
            scratch=[
                pltpu.SMEM((blocks,), jnp.int32),
                pltpu.VMEM((blocks, rows, width), bf16),
                pltpu.SemaphoreType.DMA,
                pltpu.SemaphoreType.DMA((blocks,)),
                pltpu.SemaphoreType.DMA((blocks * nx,)),
            ],
            far=(0, 1),
            far_out=(0,),
            vmem=60,
        )
        roots, send = lax.optimization_barrier((roots, send))
        roots = swap(roots, strides[0])
        got = exchange(send, wide).reshape(ng, nm, rows, cols)
        part = got[0].astype(f32)
        for i in range(1, ng):
            part = part + got[i].astype(f32)
        part = (part * sum_unit).astype(f16)
        base_rows = to_rows((base_t * base_unit).astype(f16))
        packed = jnp.concatenate([part, spread(base_rows, nzh)], axis=1)
        meta = jnp.concatenate([owner_slot, extent[:, 0], extent[:, 1]])
        meta, roots, packed = lax.optimization_barrier((meta, roots, packed))
        for stride in strides[1:]:
            roots = swap(roots, stride)
        roots = jnp.swapaxes(roots, 0, 1).reshape(owned, mine_cols, width)
        pieces = exchange(packed, "zh")
        base_t = from_rows(pieces[:, rows:], owned).astype(f32) * (1.0 / base_unit)
        pieces = pieces[:, :rows].astype(f32) * (1.0 / sum_unit)
        grads, sq = call(
            functools.partial(grad_kernel, owned),
            "masked_grad",
            (shape((ng, rows, cols), bf16), shape((8, cols), f32)),
            meta,
            pieces,
        )
        all_cols = exchange(grads, group)
        (packed,) = call(
            functools.partial(side_kernel, nx, owned),
            "right_side",
            [shape((nzh, rows + 16, lanes), bf16)],
            all_cols,
            roots,
            sq,
        )
        base_t, packed = lax.optimization_barrier((base_t, packed))
        bands = exchange(packed, "zh")
        precond, base, sums = call(
            left_kernel,
            "left_side",
            (shape((width, lanes), f32), shape((width, lanes), f32), shape((ng, 8, lanes), f32)),
            bands,
            left_roots,
            base_t,
        )
        sums = exchange(sums, group)
        fresh, step = call(
            functools.partial(fresh_kernel, nm, owned, slab),
            "new_weights",
            (shape((ng * nm, rows, lanes), bf16), shape((width, lanes), f32)),
            meta,
            sums,
            precond,
            base,
            scratch=[pltpu.VMEM((nm, rows, lanes), bf16), pltpu.SemaphoreType.DMA((nm // 2 * ng,))],
            far_out=(0,),
        )
        back = exchange(fresh, wide)
        lane = jnp.arange(lanes, dtype=jnp.int32)
        c = lane % mine_cols
        to = jnp.arange(nzl, dtype=jnp.int32)[:, None] * slab + (c // slab) * (slab * nzl) + c % slab
        to = to.reshape(nzl * lanes)
        from_slot = jnp.tile(lane // mine_cols, nzl)
        place = (to[None, :, None] == jnp.arange(cols, dtype=jnp.int32)) & (
            from_slot[None, :, None] == jnp.arange(owned, dtype=jnp.int32)[:, None, None]
        )
        (weights,) = call(
            functools.partial(place_kernel, nx, nm, owned),
            "blocks_in_order",
            [shape((blocks, rows, width), bf16)],
            meta,
            back,
            place.astype(bf16),
            scratch=[pltpu.VMEM((blocks, rows, width), bf16), pltpu.SemaphoreType.DMA((blocks,))],
            far_out=(0,),
        )

        step = step.reshape(width, owned, mine_cols)
        own_step = lax.dynamic_slice_in_dim(step, zh * slab, slab, 2).transpose(1, 0, 2)
        new_momentum = beta_decay * momentum + own_step
        new_master = master - step_rate * new_momentum
        return (new_momentum, new_master, weights)

    return local


def solution(mesh):
    nm = mesh.shape["mp"]
    nzl, nzh = 2, nm
    nx = mesh.shape["dp"] // (nzl * nzh)
    fine = Mesh(mesh.devices.reshape(nx, nzh, nzl, nm), ("x", "zh", "zl", "mp"))
    dp = ("x", "zh", "zl")
    slab_spec = P("mp", None, dp)
    return jax.shard_map(
        make_local(nx, nzh, nzl, nm),
        mesh=fine,
        in_specs=(
            P(dp, None, "mp", None),
            P(),
            P(),
            P("mp", None, None),
            slab_spec,
            slab_spec,
            slab_spec,
        ),
        out_specs=(slab_spec, slab_spec, P(None, "mp", None)),
        check_vma=False,
    )
```

```python
import functools

import jax
import jax.numpy as jnp
from jax import lax
from jax.experimental import pallas as pl
from jax.experimental.pallas import tpu as pltpu
from jax.sharding import Mesh, PartitionSpec as P

epsilon = 1e-06
beta_decay = 0.9
step_rate = 0.5
sum_unit = 2.0**11
base_unit = 2.0**12
f16 = jnp.float16
f32 = jnp.float32
bf16 = jnp.bfloat16
in_vmem = pl.BlockSpec(memory_space=pltpu.VMEM)
in_hbm = pl.BlockSpec(memory_space=pltpu.HBM)
in_smem = pl.BlockSpec(memory_space=pltpu.SMEM)


def exchange(value, axes):
    return lax.all_to_all(value, axes, split_axis=0, concat_axis=0, tiled=True)


def spread(value, count):
    return jnp.broadcast_to(value[None], (count,) + value.shape)


def bounds_of(slot, meta_ref):
    height, width = jnp.int32(0), jnp.int32(0)
    blocks = meta_ref.shape[0] // 3
    for b in range(blocks):
        hit = meta_ref[b] == slot
        height = jnp.where(hit, meta_ref[blocks + b], height)
        width = jnp.where(hit, meta_ref[2 * blocks + b], width)
    return height, width


def iota(shape, dim):
    return lax.broadcasted_iota(jnp.int32, shape, dim)


def send_kernel(
    nx, nm, owned, slots_ref, grads_ref, out_ref, owner_ref, held_ref, sem_slots, sem_in, sem_out
):
    blocks, rows, width = grads_ref.shape
    cols = width // nx
    slots = pltpu.make_async_copy(slots_ref, owner_ref, sem_slots)
    slots.start()
    reads = []
    for b in range(blocks):
        read = pltpu.make_async_copy(grads_ref.at[b], held_ref.at[b], sem_in.at[b])
        read.start()
        reads.append(read)
    slots.wait()
    copies = []
    for b in range(blocks):
        slot = owner_ref[b]
        owner, place = slot // owned, slot % owned
        reads[b].wait()
        for x in range(nx):
            copy = pltpu.make_async_copy(
                held_ref.at[b, :, x * cols : (x + 1) * cols],
                out_ref.at[(x * owned + place) * nm + owner],
                sem_out.at[b * nx + x],
            )
            copy.start()
            copies.append(copy)
    for copy in copies:
        copy.wait()


def grad_kernel(owned, meta_ref, pieces_ref, out_ref, sq_ref):
    _, rows, cols = pieces_ref.shape
    x, zh = lax.axis_index("x"), lax.axis_index("zh")
    zl, m = lax.axis_index("zl"), lax.axis_index("mp")
    height, width = bounds_of(m * owned + zl, meta_ref)
    total = pieces_ref[0]
    for i in range(1, pieces_ref.shape[0]):
        total = total + pieces_ref[i]
    ok = (zh * rows + iota((rows, cols), 0) < height) & (x * cols + iota((rows, cols), 1) < width)
    grad = jnp.where(ok, total, 0.0)
    sq_ref[...] = jnp.broadcast_to(jnp.sum(grad * grad, axis=0, keepdims=True), sq_ref.shape)
    low = grad.astype(bf16)
    for i in range(out_ref.shape[0]):
        out_ref[i] = low


def side_kernel(nx, owned, cols_ref, roots_ref, sq_ref, out_ref):
    nzh, height, lanes = out_ref.shape
    rows = cols_ref.shape[1]
    mine = roots_ref.shape[1]
    parts = []
    for s in range(owned):
        acc = jnp.zeros((rows, mine), f32)
        for x in range(nx):
            acc = acc + lax.dot_general(
                cols_ref[x * owned + s],
                roots_ref[s, :, x * lanes : (x + 1) * lanes],
                (((1,), (1,)), ((), ())),
                preferred_element_type=f32,
            )
        parts.append(acc)
    right = jnp.concatenate(parts, axis=1).astype(bf16)
    sq = sq_ref[...]
    first = sq.astype(bf16).astype(f32)
    second = (sq - first).astype(bf16).astype(f32)
    third = sq - first - second
    row = iota(sq.shape, 0)
    extra = jnp.where(row == 0, first, jnp.where(row == 1, second, jnp.where(row == 2, third, 0.0)))
    extra = jnp.concatenate([extra, jnp.zeros_like(extra)], axis=0).astype(bf16)
    for i in range(nzh):
        out_ref[i, :rows] = right
        out_ref[i, rows : rows + 16] = extra


def left_kernel(bands_ref, left_ref, base_t_ref, precond_ref, base_ref, sums_ref):
    nzh, _, lanes = bands_ref.shape
    owned, width, _ = left_ref.shape
    rows = width // nzh
    mine = lanes // owned
    side = bands_ref[:, :rows, :].reshape(width, lanes)
    lane = iota((width, lanes), 1)
    precond = jnp.zeros((width, lanes), f32)
    for s in range(owned):
        part = jnp.dot(left_ref[s], side, preferred_element_type=f32)
        precond = jnp.where(lane // mine == s, part, precond)
    precond_ref[...] = precond
    pre_sq = jnp.sum(precond * precond, axis=0, keepdims=True)
    extra = jnp.sum(bands_ref[:, rows : rows + 16, :].astype(f32), axis=0)
    grad_sq = jnp.sum(extra[:8], axis=0, keepdims=True)
    row = iota((8, lanes), 0)
    sums = jnp.where(row == 0, grad_sq, jnp.where(row == 1, pre_sq, 0.0))
    for i in range(sums_ref.shape[0]):
        sums_ref[i] = sums
    base_ref[...] = base_t_ref[...].T


def fresh_kernel(
    nm, owned, slab, meta_ref, sums_ref, precond_ref, base_ref, out_ref, step_ref
):
    width, lanes = precond_ref.shape
    mine = lanes // owned
    ng = sums_ref.shape[0]
    nzl = owned
    x, zl, m = lax.axis_index("x"), lax.axis_index("zl"), lax.axis_index("mp")
    lane = iota((1, lanes), 1)
    place = lane // mine
    c = lane % mine
    column = x * lanes + (c // slab) * (slab * nzl) + zl * slab + c % slab
    scale = jnp.zeros((1, lanes), f32)
    height = jnp.zeros((1, lanes), jnp.int32)
    total = jnp.sum(sums_ref[...], axis=0)
    for s in range(owned):
        grad_rows = sums_ref[s]
        for g in range(s + nzl, ng, nzl):
            grad_rows = grad_rows + sums_ref[g]
        grad_sq = jnp.sum(grad_rows[0:1], axis=1, keepdims=True)
        pre_sq = jnp.sum(jnp.where(place == s, total[1:2], 0.0), axis=1, keepdims=True)
        tall, wide = bounds_of(m * owned + s, meta_ref)
        scale = jnp.where(place == s, jnp.sqrt(grad_sq / (pre_sq + epsilon)), scale)
        height = jnp.where(place == s, jnp.where(column < wide, tall, 0), height)
    rows = width // nm
    for i in range(nm):
        at = slice(i * rows, (i + 1) * rows)
        ok = i * rows + iota((rows, lanes), 0) < height
        step = jnp.where(ok, scale * precond_ref[at], 0.0)
        step_ref[at] = step
        fresh = (base_ref[at] - step_rate * step).astype(bf16)
        for g in range(ng):
            out_ref[g * nm + i] = fresh


def place_kernel(
    nx,
    nm,
    owned,
    meta_ref,
    back_ref,
    place_ref,
    step_ref,
    momentum_ref,
    master_ref,
    out_ref,
    new_momentum_ref,
    new_master_ref,
    held_ref,
    flip_ref,
    sem,
):
    blocks, rows, width = out_ref.shape
    cols = width // nx
    copies = []
    for b in range(blocks):
        slot = meta_ref[b]
        owner, s = slot // owned, slot % owned
        lanes = []
        for zl in range(owned):
            lanes.append(
                jnp.concatenate([back_ref[(x * owned + zl) * nm + owner] for x in range(nx)], axis=0)
            )
        value = jnp.concatenate(lanes, axis=1)
        done = jnp.dot(value, place_ref[s], preferred_element_type=f32).astype(bf16)
        for x in range(nx):
            held_ref[b, :, x * cols : (x + 1) * cols] = done[x * rows : (x + 1) * rows]
        copy = pltpu.make_async_copy(held_ref.at[b], out_ref.at[b], sem.at[b])
        copy.start()
        copies.append(copy)
    _, slab, _ = momentum_ref.shape
    mine = step_ref.shape[1] // owned
    flip_ref[...] = step_ref[...].T
    zh = lax.axis_index("zh")
    for s in range(owned):
        own = flip_ref[pl.ds(pl.multiple_of(s * mine + zh * slab, slab), slab), :]
        new_momentum = beta_decay * momentum_ref[s] + own
        new_momentum_ref[s] = new_momentum
        new_master_ref[s] = master_ref[s] - step_rate * new_momentum
    for copy in copies:
        copy.wait()


def call(kernel, name, out, *args, scratch=(), far=(), far_out=(), vmem=24):
    specs = [in_smem if a.dtype == jnp.int32 else in_vmem for a in args]
    for i in far:
        specs[i] = in_hbm
    return pl.pallas_call(
        kernel,
        out_shape=out,
        in_specs=specs,
        out_specs=[in_hbm if i in far_out else in_vmem for i in range(len(out))],
        scratch_shapes=list(scratch),
        compiler_params=pltpu.CompilerParams(vmem_limit_bytes=vmem * 2**20),
        name=name,
    )(*args)


def shape(dims, dtype):
    return jax.ShapeDtypeStruct(dims, dtype)


def make_local(nx, nzh, nzl, nm):
    ng = nx * nzl
    group = ("x", "zl")
    wide = ("x", "zl", "mp")

    def to_rows(value):
        owned, slab, width = value.shape
        value = value.reshape(owned * slab, nx, width // nx)
        return jnp.swapaxes(value, 0, 1).reshape(nx * owned * slab, width // nx)

    def from_rows(value, owned):
        count, height, cols = value.shape
        slab = height // (nx * owned)
        value = value.reshape(count, nx, owned, slab, cols).transpose(2, 0, 3, 1, 4)
        return value.reshape(owned * count * slab, nx * cols)

    def swap(held, stride):
        pairs = [(i, i ^ stride) for i in range(nzh)]
        other = lax.ppermute(held, "zh", pairs)
        first = (lax.axis_index("zh") & stride) == 0
        low = jnp.where(first, held, other)
        high = jnp.where(first, other, held)
        return jnp.stack([low, high], axis=1).reshape((-1,) + held.shape[1:])

    def local(partial_grads, owner_slot, extent, left_roots, right_roots, momentum, master):
        blocks, rows, width = partial_grads.shape[1:]
        owned = left_roots.shape[0]
        slab = right_roots.shape[2]
        cols = width // nx
        mine_cols = slab * nzh
        lanes = owned * mine_cols

        roots = jnp.swapaxes(right_roots, 1, 2)[None]
        strides = [nzh >> i for i in range(1, nzh.bit_length())]
        base_t = jnp.swapaxes(master - (step_rate * beta_decay) * momentum, 1, 2)
        (send,) = call(
            functools.partial(send_kernel, nx, nm, owned),
            "blocks_to_owners",
            [shape((ng * nm, rows, cols), bf16)],
            owner_slot,
            partial_grads[0],
            scratch=[
                pltpu.SMEM((blocks,), jnp.int32),
                pltpu.VMEM((blocks, rows, width), bf16),
                pltpu.SemaphoreType.DMA,
                pltpu.SemaphoreType.DMA((blocks,)),
                pltpu.SemaphoreType.DMA((blocks * nx,)),
            ],
            far=(0, 1),
            far_out=(0,),
            vmem=60,
        )
        roots, send = lax.optimization_barrier((roots, send))
        roots = swap(roots, strides[0])
        got = exchange(send, wide).reshape(ng, nm, rows, cols)
        part = got[0].astype(f32)
        for i in range(1, ng):
            part = part + got[i].astype(f32)
        part = (part * sum_unit).astype(f16)
        base_rows = to_rows((base_t * base_unit).astype(f16))
        packed = jnp.concatenate([part, spread(base_rows, nzh)], axis=1)
        meta = jnp.concatenate([owner_slot, extent[:, 0], extent[:, 1]])
        meta, roots, packed = lax.optimization_barrier((meta, roots, packed))
        for stride in strides[1:]:
            roots = swap(roots, stride)
        roots = jnp.swapaxes(roots, 0, 1).reshape(owned, mine_cols, width)
        pieces = exchange(packed, "zh")
        base_t = from_rows(pieces[:, rows:], owned).astype(f32) * (1.0 / base_unit)
        pieces = pieces[:, :rows].astype(f32) * (1.0 / sum_unit)
        grads, sq = call(
            functools.partial(grad_kernel, owned),
            "masked_grad",
            (shape((ng, rows, cols), bf16), shape((8, cols), f32)),
            meta,
            pieces,
        )
        all_cols = exchange(grads, group)
        (packed,) = call(
            functools.partial(side_kernel, nx, owned),
            "right_side",
            [shape((nzh, rows + 16, lanes), bf16)],
            all_cols,
            roots,
            sq,
        )
        lane = jnp.arange(lanes, dtype=jnp.int32)
        c = lane % mine_cols
        to = jnp.arange(nzl, dtype=jnp.int32)[:, None] * slab + (c // slab) * (slab * nzl) + c % slab
        to = to.reshape(nzl * lanes)
        from_slot = jnp.tile(lane // mine_cols, nzl)
        place = (to[None, :, None] == jnp.arange(cols, dtype=jnp.int32)) & (
            from_slot[None, :, None] == jnp.arange(owned, dtype=jnp.int32)[:, None, None]
        )
        place = place.astype(bf16)
        base_t, place, packed = lax.optimization_barrier((base_t, place, packed))
        bands = exchange(packed, "zh")
        precond, base, sums = call(
            left_kernel,
            "left_side",
            (shape((width, lanes), f32), shape((width, lanes), f32), shape((ng, 8, lanes), f32)),
            bands,
            left_roots,
            base_t,
        )
        sums = exchange(sums, group)
        fresh, step = call(
            functools.partial(fresh_kernel, nm, owned, slab),
            "new_weights",
            (shape((ng * nm, rows, lanes), bf16), shape((width, lanes), f32)),
            meta,
            sums,
            precond,
            base,
        )
        back = exchange(fresh, wide)
        weights, new_momentum, new_master = call(
            functools.partial(place_kernel, nx, nm, owned),
            "blocks_in_order",
            (
                shape((blocks, rows, width), bf16),
                shape((owned, slab, width), f32),
                shape((owned, slab, width), f32),
            ),
            meta,
            back,
            place,
            step,
            jnp.swapaxes(momentum, 1, 2),
            jnp.swapaxes(master, 1, 2),
            scratch=[
                pltpu.VMEM((blocks, rows, width), bf16),
                pltpu.VMEM((lanes, width), f32),
                pltpu.SemaphoreType.DMA((blocks,)),
            ],
            far_out=(0,),
        )
        return (jnp.swapaxes(new_momentum, 1, 2), jnp.swapaxes(new_master, 1, 2), weights)

    return local


def solution(mesh):
    nm = mesh.shape["mp"]
    nzl, nzh = 2, nm
    nx = mesh.shape["dp"] // (nzl * nzh)
    fine = Mesh(mesh.devices.reshape(nx, nzh, nzl, nm), ("x", "zh", "zl", "mp"))
    dp = ("x", "zh", "zl")
    slab_spec = P("mp", None, dp)
    return jax.shard_map(
        make_local(nx, nzh, nzl, nm),
        mesh=fine,
        in_specs=(
            P(dp, None, "mp", None),
            P(),
            P(),
            P("mp", None, None),
            slab_spec,
            slab_spec,
            slab_spec,
        ),
        out_specs=(slab_spec, slab_spec, P(None, "mp", None)),
        check_vma=False,
    )
```

```python
import functools

import jax
import jax.numpy as jnp
from jax import lax
from jax.experimental import pallas as pl
from jax.experimental.pallas import tpu as pltpu
from jax.sharding import Mesh, PartitionSpec as P

epsilon = 1e-06
beta_decay = 0.9
step_rate = 0.5
sum_unit = 2.0**11
base_unit = 2.0**12
f16 = jnp.float16
f32 = jnp.float32
bf16 = jnp.bfloat16
in_vmem = pl.BlockSpec(memory_space=pltpu.VMEM)
in_hbm = pl.BlockSpec(memory_space=pltpu.HBM)
in_smem = pl.BlockSpec(memory_space=pltpu.SMEM)


def exchange(value, axes):
    return lax.all_to_all(value, axes, split_axis=0, concat_axis=0, tiled=True)


def spread(value, count):
    return jnp.broadcast_to(value[None], (count,) + value.shape)


def bounds_of(slot, meta_ref):
    height, width = jnp.int32(0), jnp.int32(0)
    blocks = meta_ref.shape[0] // 3
    for b in range(blocks):
        hit = meta_ref[b] == slot
        height = jnp.where(hit, meta_ref[blocks + b], height)
        width = jnp.where(hit, meta_ref[2 * blocks + b], width)
    return height, width


def iota(shape, dim):
    return lax.broadcasted_iota(jnp.int32, shape, dim)


def send_kernel(
    nx, nm, owned, slots_ref, grads_ref, out_ref, owner_ref, held_ref, sem_slots, sem_in, sem_out
):
    blocks, rows, width = grads_ref.shape
    cols = width // nx
    slots = pltpu.make_async_copy(slots_ref, owner_ref, sem_slots)
    slots.start()
    reads = []
    for b in range(blocks):
        read = pltpu.make_async_copy(grads_ref.at[b], held_ref.at[b], sem_in.at[b])
        read.start()
        reads.append(read)
    slots.wait()
    copies = []
    for b in range(blocks):
        slot = owner_ref[b]
        owner, place = slot // owned, slot % owned
        reads[b].wait()
        for x in range(nx):
            copy = pltpu.make_async_copy(
                held_ref.at[b, :, x * cols : (x + 1) * cols],
                out_ref.at[(x * owned + place) * nm + owner],
                sem_out.at[b * nx + x],
            )
            copy.start()
            copies.append(copy)
    for copy in copies:
        copy.wait()


def grad_kernel(owned, meta_ref, pieces_ref, out_ref, sq_ref):
    _, rows, cols = pieces_ref.shape
    x, zh = lax.axis_index("x"), lax.axis_index("zh")
    zl, m = lax.axis_index("zl"), lax.axis_index("mp")
    height, width = bounds_of(m * owned + zl, meta_ref)
    total = pieces_ref[0]
    for i in range(1, pieces_ref.shape[0]):
        total = total + pieces_ref[i]
    ok = (zh * rows + iota((rows, cols), 0) < height) & (x * cols + iota((rows, cols), 1) < width)
    grad = jnp.where(ok, total, 0.0)
    sq_ref[...] = jnp.broadcast_to(jnp.sum(grad * grad, axis=0, keepdims=True), sq_ref.shape)
    low = grad.astype(bf16)
    for i in range(out_ref.shape[0]):
        out_ref[i] = low


def side_kernel(nx, owned, cols_ref, roots_ref, sq_ref, out_ref):
    nzh, height, lanes = out_ref.shape
    rows = cols_ref.shape[1]
    mine = roots_ref.shape[1]
    parts = []
    for s in range(owned):
        acc = jnp.zeros((rows, mine), f32)
        for x in range(nx):
            acc = acc + lax.dot_general(
                cols_ref[x * owned + s],
                roots_ref[s, :, x * lanes : (x + 1) * lanes],
                (((1,), (1,)), ((), ())),
                preferred_element_type=f32,
            )
        parts.append(acc)
    right = jnp.concatenate(parts, axis=1).astype(bf16)
    sq = sq_ref[...]
    first = sq.astype(bf16).astype(f32)
    second = (sq - first).astype(bf16).astype(f32)
    third = sq - first - second
    row = iota(sq.shape, 0)
    extra = jnp.where(row == 0, first, jnp.where(row == 1, second, jnp.where(row == 2, third, 0.0)))
    extra = jnp.concatenate([extra, jnp.zeros_like(extra)], axis=0).astype(bf16)
    for i in range(nzh):
        out_ref[i, :rows] = right
        out_ref[i, rows : rows + 16] = extra


def left_kernel(bands_ref, left_ref, base_t_ref, precond_ref, base_ref, sums_ref):
    nzh, _, lanes = bands_ref.shape
    owned, width, _ = left_ref.shape
    rows = width // nzh
    mine = lanes // owned
    side = bands_ref[:, :rows, :].reshape(width, lanes)
    lane = iota((width, lanes), 1)
    precond = jnp.zeros((width, lanes), f32)
    for s in range(owned):
        part = jnp.dot(left_ref[s], side, preferred_element_type=f32)
        precond = jnp.where(lane // mine == s, part, precond)
    precond_ref[...] = precond
    pre_sq = jnp.sum(precond * precond, axis=0, keepdims=True)
    extra = jnp.sum(bands_ref[:, rows : rows + 16, :].astype(f32), axis=0)
    grad_sq = jnp.sum(extra[:8], axis=0, keepdims=True)
    row = iota((8, lanes), 0)
    sums = jnp.where(row == 0, grad_sq, jnp.where(row == 1, pre_sq, 0.0))
    for i in range(sums_ref.shape[0]):
        sums_ref[i] = sums
    base_ref[...] = base_t_ref[...].T


def fresh_kernel(
    nm, owned, slab, meta_ref, sums_ref, precond_ref, base_ref, out_ref, step_ref
):
    width, lanes = precond_ref.shape
    mine = lanes // owned
    ng = sums_ref.shape[0]
    nzl = owned
    x, zl, m = lax.axis_index("x"), lax.axis_index("zl"), lax.axis_index("mp")
    lane = iota((1, lanes), 1)
    place = lane // mine
    c = lane % mine
    column = x * lanes + (c // slab) * (slab * nzl) + zl * slab + c % slab
    scale = jnp.zeros((1, lanes), f32)
    height = jnp.zeros((1, lanes), jnp.int32)
    total = jnp.sum(sums_ref[...], axis=0)
    for s in range(owned):
        grad_rows = sums_ref[s]
        for g in range(s + nzl, ng, nzl):
            grad_rows = grad_rows + sums_ref[g]
        grad_sq = jnp.sum(grad_rows[0:1], axis=1, keepdims=True)
        pre_sq = jnp.sum(jnp.where(place == s, total[1:2], 0.0), axis=1, keepdims=True)
        tall, wide = bounds_of(m * owned + s, meta_ref)
        scale = jnp.where(place == s, jnp.sqrt(grad_sq / (pre_sq + epsilon)), scale)
        height = jnp.where(place == s, jnp.where(column < wide, tall, 0), height)
    rows = width // nm
    for i in range(nm):
        at = slice(i * rows, (i + 1) * rows)
        ok = i * rows + iota((rows, lanes), 0) < height
        step = jnp.where(ok, scale * precond_ref[at], 0.0)
        step_ref[at] = step
        fresh = (base_ref[at] - step_rate * step).astype(bf16)
        for g in range(ng):
            out_ref[g * nm + i] = fresh


def place_kernel(
    nx,
    nm,
    owned,
    meta_ref,
    back_ref,
    place_ref,
    step_ref,
    momentum_ref,
    master_ref,
    out_ref,
    new_momentum_ref,
    new_master_ref,
    held_ref,
    flip_ref,
    held_momentum_ref,
    held_master_ref,
    sem,
):
    blocks, rows, width = out_ref.shape
    cols = width // nx
    _, slab, _ = momentum_ref.shape
    mine = step_ref.shape[1] // owned
    flip_ref[...] = step_ref[...].T
    zh = lax.axis_index("zh")
    for s in range(owned):
        own = flip_ref[pl.ds(pl.multiple_of(s * mine + zh * slab, slab), slab), :]
        new_momentum = beta_decay * momentum_ref[s] + own
        held_momentum_ref[s] = new_momentum
        held_master_ref[s] = master_ref[s] - step_rate * new_momentum
    copies = [
        pltpu.make_async_copy(held_momentum_ref, new_momentum_ref, sem.at[blocks]),
        pltpu.make_async_copy(held_master_ref, new_master_ref, sem.at[blocks + 1]),
    ]
    for copy in copies:
        copy.start()
    for b in range(blocks):
        slot = meta_ref[b]
        owner, s = slot // owned, slot % owned
        lanes = []
        for zl in range(owned):
            lanes.append(
                jnp.concatenate([back_ref[(x * owned + zl) * nm + owner] for x in range(nx)], axis=0)
            )
        value = jnp.concatenate(lanes, axis=1)
        done = jnp.dot(value, place_ref[s], preferred_element_type=f32).astype(bf16)
        for x in range(nx):
            held_ref[b, :, x * cols : (x + 1) * cols] = done[x * rows : (x + 1) * rows]
        copy = pltpu.make_async_copy(held_ref.at[b], out_ref.at[b], sem.at[b])
        copy.start()
        copies.append(copy)
    for copy in copies:
        copy.wait()


def call(kernel, name, out, *args, scratch=(), far=(), far_out=(), vmem=24):
    specs = [in_smem if a.dtype == jnp.int32 else in_vmem for a in args]
    for i in far:
        specs[i] = in_hbm
    return pl.pallas_call(
        kernel,
        out_shape=out,
        in_specs=specs,
        out_specs=[in_hbm if i in far_out else in_vmem for i in range(len(out))],
        scratch_shapes=list(scratch),
        compiler_params=pltpu.CompilerParams(vmem_limit_bytes=vmem * 2**20),
        name=name,
    )(*args)


def shape(dims, dtype):
    return jax.ShapeDtypeStruct(dims, dtype)


def make_local(nx, nzh, nzl, nm):
    ng = nx * nzl
    group = ("x", "zl")
    wide = ("x", "zl", "mp")

    def to_rows(value):
        owned, slab, width = value.shape
        value = value.reshape(owned * slab, nx, width // nx)
        return jnp.swapaxes(value, 0, 1).reshape(nx * owned * slab, width // nx)

    def from_rows(value, owned):
        count, height, cols = value.shape
        slab = height // (nx * owned)
        value = value.reshape(count, nx, owned, slab, cols).transpose(2, 0, 3, 1, 4)
        return value.reshape(owned * count * slab, nx * cols)

    def swap(held, stride):
        pairs = [(i, i ^ stride) for i in range(nzh)]
        other = lax.ppermute(held, "zh", pairs)
        first = (lax.axis_index("zh") & stride) == 0
        low = jnp.where(first, held, other)
        high = jnp.where(first, other, held)
        return jnp.stack([low, high], axis=1).reshape((-1,) + held.shape[1:])

    def local(partial_grads, owner_slot, extent, left_roots, right_roots, momentum, master):
        blocks, rows, width = partial_grads.shape[1:]
        owned = left_roots.shape[0]
        slab = right_roots.shape[2]
        cols = width // nx
        mine_cols = slab * nzh
        lanes = owned * mine_cols

        roots = jnp.swapaxes(right_roots, 1, 2)[None]
        strides = [nzh >> i for i in range(1, nzh.bit_length())]
        base_t = jnp.swapaxes(master - (step_rate * beta_decay) * momentum, 1, 2)
        (send,) = call(
            functools.partial(send_kernel, nx, nm, owned),
            "blocks_to_owners",
            [shape((ng * nm, rows, cols), bf16)],
            owner_slot,
            partial_grads[0],
            scratch=[
                pltpu.SMEM((blocks,), jnp.int32),
                pltpu.VMEM((blocks, rows, width), bf16),
                pltpu.SemaphoreType.DMA,
                pltpu.SemaphoreType.DMA((blocks,)),
                pltpu.SemaphoreType.DMA((blocks * nx,)),
            ],
            far=(0, 1),
            far_out=(0,),
            vmem=60,
        )
        roots, send = lax.optimization_barrier((roots, send))
        roots = swap(roots, strides[0])
        got = exchange(send, wide).reshape(ng, nm, rows, cols)
        part = got[0].astype(f32)
        for i in range(1, ng):
            part = part + got[i].astype(f32)
        part = (part * sum_unit).astype(f16)
        base_rows = to_rows((base_t * base_unit).astype(f16))
        packed = jnp.concatenate([part, spread(base_rows, nzh)], axis=1)
        meta = jnp.concatenate([owner_slot, extent[:, 0], extent[:, 1]])
        meta, roots, packed = lax.optimization_barrier((meta, roots, packed))
        for stride in strides[1:]:
            roots = swap(roots, stride)
        roots = jnp.swapaxes(roots, 0, 1).reshape(owned, mine_cols, width)
        pieces = exchange(packed, "zh")
        base_t = from_rows(pieces[:, rows:], owned).astype(f32) * (1.0 / base_unit)
        pieces = pieces[:, :rows].astype(f32) * (1.0 / sum_unit)
        grads, sq = call(
            functools.partial(grad_kernel, owned),
            "masked_grad",
            (shape((ng, rows, cols), bf16), shape((8, cols), f32)),
            meta,
            pieces,
        )
        all_cols = exchange(grads, group)
        (packed,) = call(
            functools.partial(side_kernel, nx, owned),
            "right_side",
            [shape((nzh, rows + 16, lanes), bf16)],
            all_cols,
            roots,
            sq,
        )
        lane = jnp.arange(lanes, dtype=jnp.int32)
        c = lane % mine_cols
        to = jnp.arange(nzl, dtype=jnp.int32)[:, None] * slab + (c // slab) * (slab * nzl) + c % slab
        to = to.reshape(nzl * lanes)
        from_slot = jnp.tile(lane // mine_cols, nzl)
        place = (to[None, :, None] == jnp.arange(cols, dtype=jnp.int32)) & (
            from_slot[None, :, None] == jnp.arange(owned, dtype=jnp.int32)[:, None, None]
        )
        place = place.astype(bf16)
        base_t, place, packed = lax.optimization_barrier((base_t, place, packed))
        bands = exchange(packed, "zh")
        precond, base, sums = call(
            left_kernel,
            "left_side",
            (shape((width, lanes), f32), shape((width, lanes), f32), shape((ng, 8, lanes), f32)),
            bands,
            left_roots,
            base_t,
        )
        sums = exchange(sums, group)
        fresh, step = call(
            functools.partial(fresh_kernel, nm, owned, slab),
            "new_weights",
            (shape((ng * nm, rows, lanes), bf16), shape((width, lanes), f32)),
            meta,
            sums,
            precond,
            base,
        )
        back = exchange(fresh, wide)
        weights, new_momentum, new_master = call(
            functools.partial(place_kernel, nx, nm, owned),
            "blocks_in_order",
            (
                shape((blocks, rows, width), bf16),
                shape((owned, slab, width), f32),
                shape((owned, slab, width), f32),
            ),
            meta,
            back,
            place,
            step,
            jnp.swapaxes(momentum, 1, 2),
            jnp.swapaxes(master, 1, 2),
            scratch=[
                pltpu.VMEM((blocks, rows, width), bf16),
                pltpu.VMEM((lanes, width), f32),
                pltpu.VMEM((owned, slab, width), f32),
                pltpu.VMEM((owned, slab, width), f32),
                pltpu.SemaphoreType.DMA((blocks + 2,)),
            ],
            far_out=(0, 1, 2),
        )
        return (jnp.swapaxes(new_momentum, 1, 2), jnp.swapaxes(new_master, 1, 2), weights)

    return local


def solution(mesh):
    nm = mesh.shape["mp"]
    nzl, nzh = 2, nm
    nx = mesh.shape["dp"] // (nzl * nzh)
    fine = Mesh(mesh.devices.reshape(nx, nzh, nzl, nm), ("x", "zh", "zl", "mp"))
    dp = ("x", "zh", "zl")
    slab_spec = P("mp", None, dp)
    return jax.shard_map(
        make_local(nx, nzh, nzl, nm),
        mesh=fine,
        in_specs=(
            P(dp, None, "mp", None),
            P(),
            P(),
            P("mp", None, None),
            slab_spec,
            slab_spec,
            slab_spec,
        ),
        out_specs=(slab_spec, slab_spec, P(None, "mp", None)),
        check_vma=False,
    )
```
